32 devices in a mesh: groups: 2 (over y), space: 16 (over z, x, core).
Axes of the slice: x: 2, y: 2, z: 4, core: 2. Of those that a mesh axis runs over, the one named last changes fastest.
Arguments:
- field: bfloat16 [32, 96, 96, 128], P(('groups', 'space')), parts along dimension 0, may hold values from -6 to 6
- cotangent: bfloat16 [32, 96, 96, 128], P(('groups', 'space')), parts along dimension 0, may hold values from -6 to 6
- spectral_weight: bfloat16 [4608, 24, 128], P('space'), may hold values from -6 to 6
- skip_weight: bfloat16 [8, 8], replicated, may hold values from -2 to 2
- bias: bfloat16 [8], replicated, may hold values from -3 to 3
Outputs:
- output: bfloat16 [32, 96, 96, 128], P(('groups', 'space')), parts along dimension 0
- field_grad: bfloat16 [32, 96, 96, 128], P(('groups', 'space')), parts along dimension 0
- spectral_grad: float32 [9216, 24, 128], P(('groups', 'space')), parts along dimension 0
- skip_grad: float32 [16, 8], P('groups'), parts along dimension 0
- bias_grad: float32 [16], P('groups'), parts along dimension 0
The draws below stay inside these ranges and needn't reach their ends.
There are 2 independent parts, one for each index of `groups`. The reference program is written for one: setup_inputs(seed, part) draws one part's arguments, and reference() takes and returns one part's arrays. A program takes and returns all parts, laid end to end along the dimension named above; an argument that names none is the same for every part. Nothing has to cross between parts.
All inputs are finite; a program needn't handle non-finite values.
Results may differ from the reference program's by a relative error of at most 0.008.
Values sent between devices are 32-bit elements; how exact they have to be, the bound alone decides.
A program may use at most 128 MiB of HBM per device.

```python
import math
import jax
import jax.numpy as jnp
from jax import lax

C = 8
NT = 16
NY = 96
NZ = 96
KX = 24
KY = 24
KZ = 24
KT = 8
NX = 16
MODES = 4608


def block_levels(rng, dims, shards, least, top_value):
    level, own = 1.0, jax.random.fold_in(rng, 6)
    for dim, blocks in shards:
        draws = jnp.exp(jax.random.uniform(jax.random.fold_in(own, dim), (blocks,), jnp.float32, least / len(shards), top_value / len(shards)))
        level = level * jnp.repeat(draws, dims[dim] // blocks).reshape([-1 if axis == dim else 1 for axis in range(len(dims))])
    return level


def gaussian(own_key, dims, width, reach, shards=(), kind=jnp.bfloat16):
    array = jax.random.normal(own_key, dims, jnp.float32) * width
    if len(shards) > 0:
        array = block_levels(own_key, dims, shards, -0.22, 0.18) * array
    return jnp.clip(array, min=-reach, max=reach).astype(kind)


def setup_inputs(seed: int = 0, part: int = 0) -> dict:
    key_of = jax.random.split(jax.random.key(seed), 6)
    own_keys = jax.random.split(jax.random.fold_in(key_of[5], part), 6)
    return {
        "field": gaussian(own_keys[0], (NX, NY, NZ, NT * C), 1.0, 6.0, ((0, 16),)),
        "cotangent": gaussian(own_keys[1], (NX, NY, NZ, NT * C), 1.0, 6.0, ((0, 16),)),
        "spectral_weight": gaussian(key_of[2], (MODES, KX, 2 * C * C), 1.0, 6.0, ((0, 16),)),
        "skip_weight": gaussian(key_of[3], (C, C), C ** -0.5, 2.0),
        "bias": gaussian(key_of[4], (C,), 0.5, 3.0),
    }


FULL_PRECISION = lax.Precision.HIGHEST

def angle_pair(freqs, positions, length):
    product = freqs[:, None] * positions[None, :] % length
    angles = product.astype(jnp.float32) * (2.0 * math.pi / length)
    return (jnp.cos(angles), jnp.sin(angles))

def centred(count):
    return jnp.arange(count, dtype=jnp.int32) - count // 2

def along_x(planes, positions, length):
    channels = planes.shape[2] // 2
    cosine_x, sine_x = angle_pair(centred(KX), positions, length)
    real_part = planes[..., :channels]
    imag_part = planes[..., channels:]
    real_k = jnp.einsum('kx,xmc->mkc', cosine_x, real_part, precision=FULL_PRECISION) + jnp.einsum('kx,xmc->mkc', sine_x, imag_part, precision=FULL_PRECISION)
    imag_k = jnp.einsum('kx,xmc->mkc', cosine_x, imag_part, precision=FULL_PRECISION) - jnp.einsum('kx,xmc->mkc', sine_x, real_part, precision=FULL_PRECISION)
    return jnp.concatenate([real_k, imag_k], axis=2)

def back_along_x(spectra, positions, length):
    channels = spectra.shape[2] // 2
    cosine_x, sine_x = angle_pair(centred(KX), positions, length)
    real_part = spectra[..., :channels]
    imag_part = spectra[..., channels:]
    real_x = jnp.einsum('kx,mkc->xmc', cosine_x, real_part, precision=FULL_PRECISION) - jnp.einsum('kx,mkc->xmc', sine_x, imag_part, precision=FULL_PRECISION)
    imag_x = jnp.einsum('kx,mkc->xmc', cosine_x, imag_part, precision=FULL_PRECISION) + jnp.einsum('kx,mkc->xmc', sine_x, real_part, precision=FULL_PRECISION)
    return jnp.concatenate([real_x, imag_x], axis=2)

def split_weight(weights):
    modes, freqs, _ = weights.shape
    shaped = weights.reshape(modes, freqs, 2, C, C)
    return (shaped[:, :, 0], shaped[:, :, 1])

def mix_forward(spectra, weights):
    channels = spectra.shape[2] // 2
    weight_real, weight_imag = split_weight(weights)
    real_part = spectra[..., :channels]
    imag_part = spectra[..., channels:]
    out_real = jnp.einsum('mki,mkio->mko', real_part, weight_real, precision=FULL_PRECISION) - jnp.einsum('mki,mkio->mko', imag_part, weight_imag, precision=FULL_PRECISION)
    out_imag = jnp.einsum('mki,mkio->mko', real_part, weight_imag, precision=FULL_PRECISION) + jnp.einsum('mki,mkio->mko', imag_part, weight_real, precision=FULL_PRECISION)
    return jnp.concatenate([out_real, out_imag], axis=2)

def mix_adjoint(spectra, weights):
    channels = spectra.shape[2] // 2
    weight_real, weight_imag = split_weight(weights)
    real_part = spectra[..., :channels]
    imag_part = spectra[..., channels:]
    out_real = jnp.einsum('mko,mkio->mki', real_part, weight_real, precision=FULL_PRECISION) + jnp.einsum('mko,mkio->mki', imag_part, weight_imag, precision=FULL_PRECISION)
    out_imag = jnp.einsum('mko,mkio->mki', imag_part, weight_real, precision=FULL_PRECISION) - jnp.einsum('mko,mkio->mki', real_part, weight_imag, precision=FULL_PRECISION)
    return jnp.concatenate([out_real, out_imag], axis=2)

def weight_gradient(source, target):
    modes, freqs, double = source.shape
    channels = double // 2
    src_real = source[..., :channels]
    src_imag = source[..., channels:]
    tgt_real = target[..., :channels]
    tgt_imag = target[..., channels:]
    real_w = jnp.einsum('mki,mko->mkio', src_real, tgt_real, precision=FULL_PRECISION) + jnp.einsum('mki,mko->mkio', src_imag, tgt_imag, precision=FULL_PRECISION)
    imag_w = jnp.einsum('mki,mko->mkio', src_real, tgt_imag, precision=FULL_PRECISION) - jnp.einsum('mki,mko->mkio', src_imag, tgt_real, precision=FULL_PRECISION)
    return jnp.stack([real_w, imag_w], axis=2).reshape(modes, freqs, 2 * channels * channels)

def gelu_slope(values):
    normal_cdf = 0.5 * (1.0 + jax.scipy.special.erf(values * (1.0 / math.sqrt(2.0))))
    normal_pdf = jnp.exp(-0.5 * values * values) * (1.0 / math.sqrt(2.0 * math.pi))
    return normal_cdf + values * normal_pdf

def reference(field, cotangent, spectral_weight, skip_weight, bias):
    total = NX * NY * NZ * NT
    cosine_t, sine_t = angle_pair(jnp.arange(KT, dtype=jnp.int32), jnp.arange(NT, dtype=jnp.int32), NT)
    time_rounded = jnp.stack([cosine_t.T, -sine_t.T], axis=2).astype(jnp.bfloat16)
    time_base = lax.optimization_barrier(time_rounded).astype(jnp.float32)
    inverse_base = jnp.stack([cosine_t, -sine_t], axis=1) / total
    cosine_z, sine_z = angle_pair(centred(KZ), jnp.arange(NZ, dtype=jnp.int32), NZ)
    cosine_y, sine_y = angle_pair(centred(KY), jnp.arange(NY, dtype=jnp.int32), NY)
    skip_f32 = skip_weight.astype(jnp.float32)
    bias_f32 = bias.astype(jnp.float32)
    weight_f32 = spectral_weight.astype(jnp.float32)
    every_x = jnp.arange(NX, dtype=jnp.int32)

    def plane_spectrum(plane):
        values = plane.astype(jnp.float32).reshape(NY, NZ, NT, C)
        mixed_t = jnp.einsum('yztc,tkr->yzkrc', values, time_base, precision=FULL_PRECISION)
        real_part = mixed_t[:, :, :, 0, :]
        imag_part = mixed_t[:, :, :, 1, :]
        real_z = jnp.einsum('kz,yztc->yktc', cosine_z, real_part, precision=FULL_PRECISION) + jnp.einsum('kz,yztc->yktc', sine_z, imag_part, precision=FULL_PRECISION)
        imag_z = jnp.einsum('kz,yztc->yktc', cosine_z, imag_part, precision=FULL_PRECISION) - jnp.einsum('kz,yztc->yktc', sine_z, real_part, precision=FULL_PRECISION)
        real_y = jnp.einsum('jy,yktc->jktc', cosine_y, real_z, precision=FULL_PRECISION) + jnp.einsum('jy,yktc->jktc', sine_y, imag_z, precision=FULL_PRECISION)
        imag_y = jnp.einsum('jy,yktc->jktc', cosine_y, imag_z, precision=FULL_PRECISION) - jnp.einsum('jy,yktc->jktc', sine_y, real_z, precision=FULL_PRECISION)
        return jnp.stack([real_y, imag_y], axis=3).reshape(MODES, 2 * C)

    def plane_field(spectrum):
        grid = spectrum.reshape(KY, KZ, KT, 2, C)
        real_part = grid[:, :, :, 0, :]
        imag_part = grid[:, :, :, 1, :]
        real_y = jnp.einsum('jy,jktc->yktc', cosine_y, real_part, precision=FULL_PRECISION) - jnp.einsum('jy,jktc->yktc', sine_y, imag_part, precision=FULL_PRECISION)
        imag_y = jnp.einsum('jy,jktc->yktc', cosine_y, imag_part, precision=FULL_PRECISION) + jnp.einsum('jy,jktc->yktc', sine_y, real_part, precision=FULL_PRECISION)
        real_z = jnp.einsum('kz,yktc->yztc', cosine_z, real_y, precision=FULL_PRECISION) - jnp.einsum('kz,yktc->yztc', sine_z, imag_y, precision=FULL_PRECISION)
        imag_z = jnp.einsum('kz,yktc->yztc', cosine_z, imag_y, precision=FULL_PRECISION) + jnp.einsum('kz,yktc->yztc', sine_z, real_y, precision=FULL_PRECISION)
        stacked = jnp.stack([real_z, imag_z], axis=3)
        result = jnp.einsum('yzkrc,krt->yztc', stacked, inverse_base, precision=FULL_PRECISION)
        return result.reshape(NY, NZ, NT * C)
    own_field = along_x(lax.map(plane_spectrum, field), every_x, NX)
    back_field = back_along_x(mix_forward(own_field, weight_f32), every_x, NX)

    def forward_plane(inputs):
        plane, cot_plane, spectrum = inputs
        values = plane.astype(jnp.float32).reshape(NY, NZ, NT, C)
        skip_part = jnp.einsum('yztc,cd->yztd', values, skip_f32, precision=FULL_PRECISION).reshape(NY, NZ, NT * C)
        pre_act = plane_field(spectrum) + skip_part + jnp.tile(bias_f32, NT)
        result = jax.nn.gelu(pre_act, approximate=False).astype(jnp.bfloat16)
        grad_pre = (cot_plane.astype(jnp.float32) * gelu_slope(pre_act)).astype(jnp.bfloat16)
        return (result, grad_pre)
    output, grad_pre = lax.map(forward_plane, (field, cotangent, back_field))
    own_grad = along_x(lax.map(plane_spectrum, grad_pre), every_x, NX)
    spectral_grad = weight_gradient(own_field, own_grad / total)
    back_grad = back_along_x(mix_adjoint(own_grad, weight_f32), every_x, NX)

    def backward_plane(inputs):
        spectrum, grad_plane, plane = inputs
        grad_values = grad_plane.astype(jnp.float32).reshape(NY, NZ, NT, C)
        values = plane.astype(jnp.float32).reshape(NY, NZ, NT, C)
        skip_back = jnp.einsum('yztd,cd->yztc', grad_values, skip_f32, precision=FULL_PRECISION).reshape(NY, NZ, NT * C)
        grad_field = (plane_field(spectrum) + skip_back).astype(jnp.bfloat16)
        skip_part = jnp.einsum('yztc,yztd->cd', values, grad_values, precision=FULL_PRECISION)
        bias_part = lax.optimization_barrier(jnp.sum(grad_values, axis=(0, 1, 2)))
        return (grad_field, skip_part, bias_part)
    field_grad, skip_parts, bias_parts = lax.map(backward_plane, (back_grad, grad_pre, field))
    scale = 1.0 / math.sqrt(total)
    skip_grad = lax.optimization_barrier(jnp.sum(skip_parts, axis=0)) * scale
    bias_grad = lax.optimization_barrier(jnp.sum(bias_parts, axis=0)) * scale
    return (output, field_grad, spectral_grad, skip_grad, bias_grad)
```

```python
import functools
import math

import jax
import jax.numpy as jnp
import ml_dtypes
import numpy as np
from jax import lax
from jax.experimental import pallas as pl
from jax.experimental.pallas import tpu as pltpu
from jax.sharding import PartitionSpec as P

KX = 24
KY = 24
KZ = 24
KT = 8


FULL_PRECISION = lax.Precision.HIGHEST


def angle_pair(freqs, positions, length):
    product = freqs[:, None] * positions[None, :] % length
    angles = product.astype(jnp.float32) * (2.0 * math.pi / length)
    return (jnp.cos(angles), jnp.sin(angles))


def centred(count):
    return jnp.arange(count, dtype=jnp.int32) - count // 2


def kron_eye(base, channels):
    eye_matrix = jnp.eye(channels, dtype=jnp.float32)
    rows_in, cols_in = base.shape
    return (base[:, None, :, None] * eye_matrix[None, :, None, :]).reshape(
        rows_in * channels, cols_in * channels
    )


def block_diagonal(weight, copies):
    eye_matrix = jnp.eye(copies, dtype=jnp.float32)
    width_in, width_out = weight.shape
    return (eye_matrix[:, None, :, None] * weight[None, :, None, :]).reshape(
        copies * width_in, copies * width_out
    )


def turned_forward(values):
    half = values.shape[-1] // 2
    return jnp.concatenate([values[..., half:], -values[..., :half]], axis=-1)


def turned_back(values):
    half = values.shape[-1] // 2
    return jnp.concatenate([-values[..., half:], values[..., :half]], axis=-1)


def plane_spectra(values, time_table, channels):
    cells_x, rows_y, rows_z, _ = values.shape
    mixed_t = jnp.dot(values, time_table, preferred_element_type=jnp.float32)
    cosine_z, sine_z = angle_pair(centred(KZ), jnp.arange(rows_z, dtype=jnp.int32), rows_z)
    table_z = jnp.concatenate([cosine_z, sine_z], axis=1)
    stacked_z = jnp.concatenate([mixed_t, turned_forward(mixed_t)], axis=2)
    along_z = jnp.einsum("kz,xyzm->xykm", table_z, stacked_z, precision=FULL_PRECISION)
    cosine_y, sine_y = angle_pair(centred(KY), jnp.arange(rows_y, dtype=jnp.int32), rows_y)
    table_y = jnp.concatenate([cosine_y, sine_y], axis=1)
    stacked_y = jnp.concatenate([along_z, turned_forward(along_z)], axis=1)
    along_y = jnp.einsum("jy,xykm->xjkm", table_y, stacked_y, precision=FULL_PRECISION)
    grid = along_y.reshape(cells_x, KY, KZ, 2, KT, channels).transpose(0, 1, 2, 4, 3, 5)
    return grid.reshape(cells_x, KY * KZ * KT, 2 * channels)


def plane_fields(planes, inverse_table, rows_y, rows_z):
    cells_x = planes.shape[0]
    channels = planes.shape[2] // 2
    grid = planes.reshape(cells_x, KY, KZ, KT, 2, channels).transpose(0, 1, 2, 4, 3, 5)
    grid = grid.reshape(cells_x, KY, KZ, 2 * KT * channels)
    cosine_y, sine_y = angle_pair(centred(KY), jnp.arange(rows_y, dtype=jnp.int32), rows_y)
    table_y = jnp.concatenate([cosine_y.T, sine_y.T], axis=1)
    stacked_y = jnp.concatenate([grid, turned_back(grid)], axis=1)
    along_y = jnp.einsum("yj,xjkm->xykm", table_y, stacked_y, precision=FULL_PRECISION)
    timed = jnp.dot(
        along_y, inverse_table, precision=FULL_PRECISION, preferred_element_type=jnp.float32
    )
    width_out = timed.shape[3] // 2
    cosine_z, sine_z = angle_pair(centred(KZ), jnp.arange(rows_z, dtype=jnp.int32), rows_z)
    table_z = jnp.stack([cosine_z.T, -sine_z.T], axis=2).reshape(rows_z, 2 * KZ)
    paired = timed.reshape(cells_x, rows_y, 2 * KZ, width_out)
    return jnp.einsum("zk,xykm->xyzm", table_z, paired, precision=FULL_PRECISION)


def along_x(planes, positions, length):
    channels = planes.shape[2] // 2
    cosine_x, sine_x = angle_pair(centred(KX), positions, length)
    real_part = planes[..., :channels]
    imag_part = planes[..., channels:]
    real_k = jnp.einsum("kx,xmc->mkc", cosine_x, real_part, precision=FULL_PRECISION) + jnp.einsum(
        "kx,xmc->mkc", sine_x, imag_part, precision=FULL_PRECISION
    )
    imag_k = jnp.einsum("kx,xmc->mkc", cosine_x, imag_part, precision=FULL_PRECISION) - jnp.einsum(
        "kx,xmc->mkc", sine_x, real_part, precision=FULL_PRECISION
    )
    return jnp.concatenate([real_k, imag_k], axis=2)


def back_along_x(spectra, positions, length):
    channels = spectra.shape[2] // 2
    cosine_x, sine_x = angle_pair(centred(KX), positions, length)
    real_part = spectra[..., :channels]
    imag_part = spectra[..., channels:]
    real_x = jnp.einsum("kx,mkc->xmc", cosine_x, real_part, precision=FULL_PRECISION) - jnp.einsum(
        "kx,mkc->xmc", sine_x, imag_part, precision=FULL_PRECISION
    )
    imag_x = jnp.einsum("kx,mkc->xmc", cosine_x, imag_part, precision=FULL_PRECISION) + jnp.einsum(
        "kx,mkc->xmc", sine_x, real_part, precision=FULL_PRECISION
    )
    return jnp.concatenate([real_x, imag_x], axis=2)


def split_weight(weights, channels):
    modes, freqs, _ = weights.shape
    shaped = weights.reshape(modes, freqs, 2, channels, channels)
    return (shaped[:, :, 0], shaped[:, :, 1])


def mix_forward(spectra, weights):
    channels = spectra.shape[2] // 2
    weight_real, weight_imag = split_weight(weights, channels)
    real_part = spectra[..., :channels]
    imag_part = spectra[..., channels:]
    out_real = jnp.einsum(
        "mki,mkio->mko", real_part, weight_real, precision=FULL_PRECISION
    ) - jnp.einsum("mki,mkio->mko", imag_part, weight_imag, precision=FULL_PRECISION)
    out_imag = jnp.einsum(
        "mki,mkio->mko", real_part, weight_imag, precision=FULL_PRECISION
    ) + jnp.einsum("mki,mkio->mko", imag_part, weight_real, precision=FULL_PRECISION)
    return jnp.concatenate([out_real, out_imag], axis=2)


def mix_adjoint(spectra, weights):
    channels = spectra.shape[2] // 2
    weight_real, weight_imag = split_weight(weights, channels)
    real_part = spectra[..., :channels]
    imag_part = spectra[..., channels:]
    out_real = jnp.einsum(
        "mko,mkio->mki", real_part, weight_real, precision=FULL_PRECISION
    ) + jnp.einsum("mko,mkio->mki", imag_part, weight_imag, precision=FULL_PRECISION)
    out_imag = jnp.einsum(
        "mko,mkio->mki", imag_part, weight_real, precision=FULL_PRECISION
    ) - jnp.einsum("mko,mkio->mki", real_part, weight_imag, precision=FULL_PRECISION)
    return jnp.concatenate([out_real, out_imag], axis=2)


def weight_gradient(source, target):
    modes, freqs, double = source.shape
    channels = double // 2
    src_real = source[..., :channels]
    src_imag = source[..., channels:]
    tgt_real = target[..., :channels]
    tgt_imag = target[..., channels:]
    real_w = jnp.einsum("mki,mko->mkio", src_real, tgt_real, precision=FULL_PRECISION) + jnp.einsum(
        "mki,mko->mkio", src_imag, tgt_imag, precision=FULL_PRECISION
    )
    imag_w = jnp.einsum("mki,mko->mkio", src_real, tgt_imag, precision=FULL_PRECISION) - jnp.einsum(
        "mki,mko->mkio", src_imag, tgt_real, precision=FULL_PRECISION
    )
    return jnp.stack([real_w, imag_w], axis=2).reshape(modes, freqs, 2 * channels * channels)


def gelu_slope(values):
    normal_cdf = 0.5 * (1.0 + jax.scipy.special.erf(values * (1.0 / math.sqrt(2.0))))
    normal_pdf = jnp.exp(-0.5 * values * values) * (1.0 / math.sqrt(2.0 * math.pi))
    return normal_cdf + values * normal_pdf


def on_device(field, cotangent, spectral_weight, skip_weight, bias):
    cells_x, rows_y, rows_z, last_dim = field.shape
    channels = skip_weight.shape[0]
    steps_t = last_dim // channels
    devices = lax.axis_size("space")
    length_x = cells_x * devices
    total = length_x * rows_y * rows_z * steps_t
    every_x = jnp.arange(length_x, dtype=jnp.int32)
    cosine_t, sine_t = angle_pair(
        jnp.arange(KT, dtype=jnp.int32), jnp.arange(steps_t, dtype=jnp.int32), steps_t
    )
    forward_base = jnp.stack([cosine_t.T, -sine_t.T], axis=1).reshape(steps_t, 2 * KT)
    time_table = kron_eye(forward_base, channels).astype(jnp.bfloat16)
    upper_rows = jnp.concatenate([cosine_t, sine_t], axis=1)
    lower_rows = jnp.concatenate([-sine_t, cosine_t], axis=1)
    inverse_base = jnp.concatenate([upper_rows, lower_rows], axis=0) / total
    inverse_table = kron_eye(inverse_base, channels)
    weight_f32 = spectral_weight.astype(jnp.float32)
    skip_f32 = skip_weight.astype(jnp.float32)

    def to_owner(planes):
        arrived = lax.all_to_all(planes, "space", split_axis=1, concat_axis=0, tiled=True)
        return along_x(arrived, every_x, length_x)

    def to_planes(spectra):
        columns = back_along_x(spectra, every_x, length_x)
        return lax.all_to_all(columns, "space", split_axis=0, concat_axis=1, tiled=True)

    own_field = to_owner(plane_spectra(field, time_table, channels))
    skip_table = block_diagonal(skip_f32, steps_t).astype(jnp.bfloat16)
    skip_part = jnp.dot(field, skip_table, preferred_element_type=jnp.float32)
    spectral_part = plane_fields(
        to_planes(mix_forward(own_field, weight_f32)), inverse_table, rows_y, rows_z
    )
    pre_act = spectral_part + skip_part + jnp.tile(bias.astype(jnp.float32), steps_t)
    output = jax.nn.gelu(pre_act, approximate=False).astype(jnp.bfloat16)
    grad_pre = (cotangent.astype(jnp.float32) * gelu_slope(pre_act)).astype(jnp.bfloat16)
    own_grad = to_owner(plane_spectra(grad_pre, time_table, channels))
    skip_back = block_diagonal(skip_f32.T, steps_t).astype(jnp.bfloat16)
    local_back = jnp.dot(grad_pre, skip_back, preferred_element_type=jnp.float32)
    flat_field = field.reshape(-1, last_dim)
    flat_grad = grad_pre.reshape(-1, last_dim)
    outer_sum = lax.dot_general(
        flat_field, flat_grad, (((0,), (0,)), ((), ())), preferred_element_type=jnp.float32
    )
    local_skip = jnp.einsum("tatb->ab", outer_sum.reshape(steps_t, channels, steps_t, channels))
    local_bias = jnp.sum(flat_grad.reshape(-1, steps_t, channels), axis=(0, 1), dtype=jnp.float32)
    skip_total, bias_total = lax.psum((local_skip, local_bias), "space")
    spectral_grad = weight_gradient(own_field, own_grad / total)
    back_part = plane_fields(
        to_planes(mix_adjoint(own_grad, weight_f32)), inverse_table, rows_y, rows_z
    )
    field_grad = (back_part + local_back).astype(jnp.bfloat16)
    scale = 1.0 / math.sqrt(total)
    return (output, field_grad, spectral_grad, skip_total * scale, bias_total * scale)


PAD_ROWS = 8


def split_pair(values):
    high = values.astype(jnp.bfloat16)
    low = (values - high.astype(jnp.float32)).astype(jnp.bfloat16)
    return high, low


def dot32(left, right):
    return jnp.dot(left, right, preferred_element_type=jnp.float32)


def np_angles(freqs, positions, length):
    angles = (np.outer(freqs, positions) % length) * (2.0 * math.pi / length)
    return np.cos(angles), np.sin(angles)


def np_split(table):
    high = table.astype(np.float32).astype(ml_dtypes.bfloat16)
    low = (table - high.astype(np.float64)).astype(np.float32).astype(ml_dtypes.bfloat16)
    return high, low


def np_bf16(table):
    return table.astype(np.float32).astype(ml_dtypes.bfloat16)


def make_tables(rows_y, rows_z, steps_t, channels, devices):
    half = KT * channels
    lanes = 2 * half
    eye_c = np.eye(channels)
    cos_z, sin_z = np_angles(np.arange(KZ) - KZ // 2, np.arange(rows_z), rows_z)
    cos_y, sin_y = np_angles(np.arange(KY) - KY // 2, np.arange(rows_y), rows_y)
    cos_t, sin_t = np_angles(np.arange(KT), np.arange(steps_t), steps_t)
    cos_x, sin_x = np_angles(np.arange(KX) - KX // 2, np.arange(devices), devices)
    tables = {}
    tables["z_fwd"] = np_bf16(np.concatenate([cos_z, sin_z], 0))
    tables["y_fwd"] = np_bf16(np.concatenate([cos_y, sin_y], 0))
    time_fwd = np.kron(np.stack([cos_t.T, -sin_t.T], 1).reshape(steps_t, 2 * KT), eye_c)
    turned = np.concatenate([time_fwd[:, half:], -time_fwd[:, :half]], 1)
    tables["t_fwd"] = np_bf16(np.concatenate([time_fwd, turned], 0))
    y_high, y_low = np_split(np.concatenate([cos_y.T, sin_y.T], 1))
    tables["y_back"] = np.concatenate([y_high, y_high, y_low], 1)
    time_back = np.concatenate(
        [np.concatenate([cos_t, sin_t], 1), np.concatenate([-sin_t, cos_t], 1)], 0
    )
    tables["t_back"] = np_bf16(np.kron(time_back, eye_c))
    tables["z_back"] = np_bf16(np.concatenate([cos_z.T, -sin_z.T], 1))
    eye_p = np.eye(PAD_ROWS)

    def spread(base):
        return np.einsum("kx,pq->pkxq", base, eye_p).reshape(
            PAD_ROWS * KX, devices * PAD_ROWS
        )

    x_high, x_low = np_split(np.concatenate([spread(cos_x), spread(sin_x)], 0))
    tables["x_fwd"] = np.concatenate([x_high, x_high, x_low], 1)
    tables["x_back"] = np.concatenate(
        np_split(np.concatenate([spread(cos_x).T, spread(sin_x).T], 1)), 0
    )
    c = channels
    pick_s = np.zeros((KT, 2, KT, c, 2, 2, c, c))
    pick_t = np.zeros((KT, 2, KT, c, 2, 2, c, c))
    fold_s = np.zeros((KT, 2, 2, c, c, 2, KT, c))
    fold_t = np.zeros((KT, 2, 2, c, c, 2, KT, c))
    for k in range(KT):
        for a in range(c):
            pick_s[k, 0, k, a, 0, :, a, :] = 1
            pick_s[k, 1, k, a, 1, 0, a, :] = 1
            pick_s[k, 1, k, a, 1, 1, a, :] = -1
            pick_t[k, 0, k, a, 0, 0, :, a] = 1
            pick_t[k, 1, k, a, 0, 1, :, a] = 1
            pick_t[k, 1, k, a, 1, 0, :, a] = 1
            pick_t[k, 0, k, a, 1, 1, :, a] = 1
            fold_s[k, 0, 0, :, a, 0, k, a] = 1
            fold_s[k, 1, 1, :, a, 0, k, a] = 1
            fold_s[k, 0, 1, :, a, 1, k, a] = 1
            fold_s[k, 1, 0, :, a, 1, k, a] = 1
            fold_t[k, 0, :, a, :, 0, k, a] = 1
            fold_t[k, 1, 0, a, :, 1, k, a] = 1
            fold_t[k, 1, 1, a, :, 1, k, a] = -1
    wide = 2 * c * c

    def doubled(pick):
        flat = pick.reshape(KT, lanes, 2 * wide)
        return np_bf16(np.concatenate([flat, flat], 1))

    tables["pick_s"] = doubled(pick_s)
    tables["pick_t"] = doubled(pick_t)
    tables["fold_s"] = np_bf16(fold_s.reshape(KT, 2 * wide, lanes))
    tables["fold_t"] = np_bf16(fold_t.reshape(KT, 2 * wide, lanes))
    return {name: jnp.asarray(table) for name, table in tables.items()}


def half_sign(shape, first, second):
    lane = lax.broadcasted_iota(jnp.int32, shape, 1)
    return jnp.where(lane < shape[1] // 2, first, second).astype(jnp.float32)


def roll_half(values):
    return pltpu.roll(values, values.shape[1] // 2, 1)


def z_forward(rows, count, z_table, t_table):
    pieces = []
    for y in range(count):
        both = dot32(z_table, rows(y))
        pieces.append(jnp.concatenate([both[:KZ], both[KZ:]], axis=1))
    stacked = jnp.concatenate(pieces, axis=0).astype(jnp.bfloat16)
    return dot32(stacked, t_table)


def y_forward(zbuf, spec, y_table, rows_y, lanes):
    sign = half_sign((KY, lanes), 1.0, -1.0)
    for kz in range(KZ):
        column = zbuf[pl.ds(kz, rows_y, stride=KZ), :].astype(jnp.bfloat16)
        both = dot32(y_table, column)
        spec[pl.ds(kz, KY, stride=KZ), :] = both[:KY] + sign * roll_half(both[KY:])


def y_backward(spec, ubuf, y_table, rows_y, lanes):
    sign = half_sign((KY, lanes), -1.0, 1.0)
    for kz in range(KZ):
        column = spec[pl.ds(kz, KY, stride=KZ), :]
        both = jnp.concatenate([column, sign * roll_half(column)], axis=0)
        high, low = split_pair(both)
        stacked = jnp.concatenate([high, low, high], axis=0)
        ubuf[pl.ds(kz, rows_y, stride=KZ), :] = dot32(y_table, stacked)


def z_backward(ubuf, start, count, t_table):
    lanes = ubuf.shape[1]
    rows = ubuf[pl.ds(start, count * KZ), :].astype(jnp.bfloat16)
    timed = dot32(rows, t_table)
    pieces = []
    for y in range(count):
        mine = timed[y * KZ : (y + 1) * KZ]
        pieces.append(
            jnp.concatenate([mine[:, :lanes], mine[:, lanes:]], axis=0).astype(jnp.bfloat16)
        )
    return pieces


def write_blocks(spec, out_ref, own, stats):
    devices, padded, lanes = out_ref.shape
    spare = padded - own
    if spare > 1:
        zeros = jnp.zeros((spare - 1, lanes), jnp.float32)
        tail = jnp.concatenate([stats, zeros], axis=0)
    else:
        tail = stats
    for d in range(devices):
        out_ref[d, 0:own, :] = spec[d * own : (d + 1) * own, :]
        out_ref[d, own:padded, :] = tail


def read_blocks(in_ref, spec, own, scale):
    for d in range(in_ref.shape[0]):
        spec[d * own : (d + 1) * own, :] = in_ref[d, 0:own, :] * scale


def spectrum_kernel(count, own, f_ref, zt_ref, tt_ref, yt_ref, out_ref, zbuf, spec):
    step = pl.program_id(0)
    lanes = zbuf.shape[1]
    chunk = z_forward(lambda y: f_ref[y], count, zt_ref[...], tt_ref[...])
    zbuf[pl.ds(pl.multiple_of(step * (count * KZ), 8), count * KZ), :] = chunk

    @pl.when(step == pl.num_programs(0) - 1)
    def _():
        y_forward(zbuf, spec, yt_ref[...], zbuf.shape[0] // KZ, lanes)
        write_blocks(spec, out_ref, own, jnp.zeros((1, lanes), jnp.float32))


def activation_kernel(
    count,
    own,
    scale,
    channels,
    in_ref,
    f_ref,
    cot_ref,
    skip_ref,
    bias_ref,
    yb_ref,
    tb_ref,
    zb_ref,
    zt_ref,
    tt_ref,
    yt_ref,
    out_ref,
    grad_ref,
    send_ref,
    ubuf,
    zbuf,
    spec,
    outer,
    total_row,
):
    step = pl.program_id(0)
    lanes = ubuf.shape[1]
    rows_y = ubuf.shape[0] // KZ

    @pl.when(step == 0)
    def _():
        read_blocks(in_ref, spec, own, scale)
        y_backward(spec, ubuf, yb_ref[...], rows_y, lanes)
        outer[...] = jnp.zeros_like(outer)
        total_row[...] = jnp.zeros_like(total_row)

    start = pl.multiple_of(step * (count * KZ), 8)
    pieces = z_backward(ubuf, start, count, tb_ref[...])
    bias_row = bias_ref[...]
    for y in range(count):
        field = f_ref[y]
        pre = dot32(zb_ref[...], pieces[y]) + dot32(field, skip_ref[...]) + bias_row
        cdf = 0.5 * (1.0 + lax.erf(pre * (1.0 / math.sqrt(2.0))))
        pdf = jnp.exp(-0.5 * pre * pre) * (1.0 / math.sqrt(2.0 * math.pi))
        out_ref[y] = (pre * cdf).astype(jnp.bfloat16)
        slope = cdf + pre * pdf
        grad = (cot_ref[y].astype(jnp.float32) * slope).astype(jnp.bfloat16)
        grad_ref[y] = grad
        total_row[...] += jnp.sum(
            grad.astype(jnp.float32).reshape(-1, 8, lanes), axis=0
        )
    flat_f = f_ref[...].reshape(-1, lanes)
    flat_g = grad_ref[...].reshape(-1, lanes)
    outer[...] += lax.dot_general(
        flat_f, flat_g, (((0,), (0,)), ((), ())), preferred_element_type=jnp.float32
    )
    chunk = z_forward(lambda y: grad_ref[y], count, zt_ref[...], tt_ref[...])
    zbuf[pl.ds(start, count * KZ), :] = chunk

    @pl.when(step == pl.num_programs(0) - 1)
    def _():
        y_forward(zbuf, spec, yt_ref[...], rows_y, lanes)
        row = lax.broadcasted_iota(jnp.int32, (lanes, lanes), 0)
        lane = lax.broadcasted_iota(jnp.int32, (lanes, lanes), 1)
        same_t = row // channels == lane // channels
        same_c = (row % channels == lane % channels).astype(jnp.float32)
        diagonal = jnp.where(same_t, outer[...], 0.0)
        per_c = jnp.dot(diagonal, same_c, precision=FULL_PRECISION)
        keep = (row % channels) == (lane // channels)
        skip_row = jnp.sum(jnp.where(keep, per_c, 0.0), axis=0, keepdims=True)
        folded = jnp.dot(total_row[...], same_c, precision=FULL_PRECISION)
        group = lax.broadcasted_iota(jnp.int32, (1, lanes), 1) // channels
        bias_sum = jnp.sum(folded, axis=0, keepdims=True)
        bias_sum = jnp.where(group == channels, bias_sum, 0.0)
        write_blocks(spec, send_ref, own, skip_row + bias_sum)


def field_grad_kernel(
    count, own, scale, in_ref, grad_ref, skip_ref, yb_ref, tb_ref, zb_ref, out_ref, ubuf, spec
):
    step = pl.program_id(0)
    lanes = ubuf.shape[1]

    @pl.when(step == 0)
    def _():
        read_blocks(in_ref, spec, own, scale)
        y_backward(spec, ubuf, yb_ref[...], ubuf.shape[0] // KZ, lanes)

    start = pl.multiple_of(step * (count * KZ), 8)
    pieces = z_backward(ubuf, start, count, tb_ref[...])
    for y in range(count):
        value = dot32(zb_ref[...], pieces[y]) + dot32(grad_ref[y], skip_ref[...])
        out_ref[y] = value.astype(jnp.bfloat16)


def x_forward(in_ref, tile, x_table):
    devices, _, lanes = in_ref.shape
    block = in_ref[:, tile * PAD_ROWS : (tile + 1) * PAD_ROWS, :]
    block = block.reshape(devices * PAD_ROWS, lanes)
    high, low = split_pair(block)
    both = dot32(x_table, jnp.concatenate([high, low, high], axis=0))
    rows = PAD_ROWS * KX
    return both[:rows] + half_sign((rows, lanes), 1.0, -1.0) * roll_half(both[rows:])


def x_backward(columns, out_ref, tile, x_table):
    devices, _, lanes = out_ref.shape
    missing = PAD_ROWS * KX - columns.shape[0]
    if missing:
        columns = jnp.concatenate([columns, jnp.zeros((missing, lanes), jnp.float32)], axis=0)
    turned = half_sign(columns.shape, -1.0, 1.0) * roll_half(columns)
    high, low = split_pair(jnp.concatenate([columns, turned], axis=0))
    size = devices * PAD_ROWS
    from_high = dot32(x_table, high)
    rows = from_high[:size] + from_high[size:] + dot32(x_table[:size], low)
    out_ref[:, tile * PAD_ROWS : (tile + 1) * PAD_ROWS, :] = rows.reshape(
        devices, PAD_ROWS, lanes
    )


def mixed_rows(spectrum, w_ref, first, pairs, pick_ref, fold_ref):
    wide = w_ref.shape[3]
    high, low = split_pair(spectrum)
    doubled = jnp.concatenate([high, low], axis=1)
    total = None
    for k in range(KT):
        terms = dot32(doubled, pick_ref[k])
        weight = w_ref[first : first + pairs, k].astype(jnp.float32).reshape(pairs * KX, wide)
        product = jnp.concatenate([terms[:, :wide] * weight, terms[:, wide:] * weight], axis=1)
        part = dot32(product.astype(jnp.bfloat16), fold_ref[k])
        total = part if total is None else total + part
    return total


def mix_kernel(with_stats, in_ref, w_ref, xf_ref, xb_ref, pick_ref, fold_ref, *outs):
    spectrum_ref, send_ref = outs[:2]
    own = w_ref.shape[0]
    rows = PAD_ROWS * KX
    for tile in range(pl.cdiv(own, PAD_ROWS)):
        first = tile * PAD_ROWS
        pairs = min(PAD_ROWS, own - first)
        spectrum = x_forward(in_ref, tile, xf_ref[...])
        spectrum_ref[tile * rows : (tile + 1) * rows, :] = spectrum
        mixed = mixed_rows(spectrum[: pairs * KX], w_ref, first, pairs, pick_ref, fold_ref)
        x_backward(mixed, send_ref, tile, xb_ref[...])
    for tile in range(pl.cdiv(own, PAD_ROWS), in_ref.shape[1] // PAD_ROWS):
        lanes = send_ref.shape[2]
        send_ref[:, tile * PAD_ROWS : (tile + 1) * PAD_ROWS, :] = jnp.zeros(
            (send_ref.shape[0], PAD_ROWS, lanes), jnp.float32
        )
    if with_stats:
        outs[2][...] = jnp.sum(in_ref[:, own, :], axis=0, keepdims=True)


def weight_gradient_kernel(scale, s_ref, t_ref, ps_ref, pt_ref, out_ref):
    pairs, _, _, wide = out_ref.shape
    for_s = jnp.concatenate(split_pair(s_ref[...]), axis=1)
    for_t = jnp.concatenate(split_pair(t_ref[...] * scale), axis=1)
    for k in range(KT):
        left = dot32(for_s, ps_ref[k])
        right = dot32(for_t, pt_ref[k])
        value = left[:, :wide] * right[:, :wide] + left[:, wide:] * right[:, wide:]
        out_ref[:, k] = value.reshape(pairs, KX, wide)


def whole(array):
    zeros = (0,) * array.ndim
    return pl.BlockSpec(array.shape, lambda *_: zeros)


def params(**extra):
    return pltpu.CompilerParams(vmem_limit_bytes=48 * 1024 * 1024, **extra)


def fast_device(field, cotangent, spectral_weight, skip_weight, bias):
    _, rows_y, rows_z, lanes = field.shape
    channels = skip_weight.shape[0]
    steps_t = lanes // channels
    devices = lax.axis_size("space")
    total = devices * rows_y * rows_z * steps_t
    scale = 1.0 / total
    own = KY * KZ // devices
    padded = (own // PAD_ROWS + 1) * PAD_ROWS
    wide = spectral_weight.shape[2]
    t = make_tables(rows_y, rows_z, steps_t, channels, devices)
    count = 16
    while rows_y % count:
        count //= 2
    steps = rows_y // count
    field = field.reshape(rows_y, rows_z, lanes)
    cotangent = cotangent.reshape(rows_y, rows_z, lanes)
    weights = spectral_weight.reshape(own, KT, KX, wide)
    skip_f32 = skip_weight.astype(jnp.float32)
    skip_table = block_diagonal(skip_f32, steps_t).astype(jnp.bfloat16)
    skip_back = block_diagonal(skip_f32.T, steps_t).astype(jnp.bfloat16)
    bias_row = jnp.tile(bias.astype(jnp.float32), steps_t).reshape(1, lanes)
    plane_spec = pl.BlockSpec((count, rows_z, lanes), lambda i: (i, 0, 0))
    plane_shape = jax.ShapeDtypeStruct((rows_y, rows_z, lanes), jnp.bfloat16)
    block_shape = jax.ShapeDtypeStruct((devices, padded, lanes), jnp.float32)
    block_spec = pl.BlockSpec((devices, padded, lanes), lambda *_: (0, 0, 0))
    mode_rows = pl.cdiv(own, PAD_ROWS) * PAD_ROWS * KX
    spectrum_shape = jax.ShapeDtypeStruct((mode_rows, lanes), jnp.float32)
    plane_buf = pltpu.VMEM((rows_y * KZ, lanes), jnp.float32)
    spec_buf = pltpu.VMEM((KY * KZ, lanes), jnp.float32)

    def exchange(blocks):
        return lax.all_to_all(blocks, "space", split_axis=0, concat_axis=0, tiled=True)

    operands = (field, t["z_fwd"], t["t_fwd"], t["y_fwd"])
    sent = pl.pallas_call(
        functools.partial(spectrum_kernel, count, own),
        grid=(steps,),
        in_specs=[plane_spec] + [whole(x) for x in operands[1:]],
        out_specs=block_spec,
        out_shape=block_shape,
        scratch_shapes=[plane_buf, spec_buf],
        compiler_params=params(),
        name="field_spectrum",
    )(*operands)
    own_field, sent = pl.pallas_call(
        functools.partial(mix_kernel, False),
        out_shape=[spectrum_shape, block_shape],
        compiler_params=params(),
        name="mix_forward",
    )(exchange(sent), weights, t["x_fwd"], t["x_back"], t["pick_s"], t["fold_s"])
    operands = (
        exchange(sent),
        field,
        cotangent,
        skip_table,
        bias_row,
        t["y_back"],
        t["t_back"],
        t["z_back"],
        t["z_fwd"],
        t["t_fwd"],
        t["y_fwd"],
    )
    output, grad_pre, sent = pl.pallas_call(
        functools.partial(activation_kernel, count, own, scale, channels),
        grid=(steps,),
        in_specs=[whole(operands[0]), plane_spec, plane_spec] + [whole(x) for x in operands[3:]],
        out_specs=[plane_spec, plane_spec, block_spec],
        out_shape=[plane_shape, plane_shape, block_shape],
        scratch_shapes=[
            plane_buf,
            plane_buf,
            spec_buf,
            pltpu.VMEM((lanes, lanes), jnp.float32),
            pltpu.VMEM((8, lanes), jnp.float32),
        ],
        compiler_params=params(),
        name="activation",
    )(*operands)
    own_grad, sent, stats = pl.pallas_call(
        functools.partial(mix_kernel, True),
        out_shape=[spectrum_shape, block_shape, jax.ShapeDtypeStruct((1, lanes), jnp.float32)],
        compiler_params=params(),
        name="mix_adjoint",
    )(exchange(sent), weights, t["x_fwd"], t["x_back"], t["pick_t"], t["fold_t"])
    arrived = exchange(sent)
    pairs = 4 if own % 4 == 0 else 1
    mode_spec = pl.BlockSpec((pairs * KX, lanes), lambda i: (i, 0))
    spectral_grad = pl.pallas_call(
        functools.partial(weight_gradient_kernel, scale),
        grid=(own // pairs,),
        in_specs=[mode_spec, mode_spec, whole(t["pick_s"]), whole(t["pick_t"])],
        out_specs=pl.BlockSpec((pairs, KT, KX, wide), lambda i: (i, 0, 0, 0)),
        out_shape=jax.ShapeDtypeStruct((own, KT, KX, wide), jnp.float32),
        compiler_params=params(),
        cost_estimate=pl.CostEstimate(
            flops=4 * own * KX * KT * 65536, bytes_accessed=8 * own * KX * KT * wide, transcendentals=0
        ),
        name="weight_gradient",
    )(own_field, own_grad, t["pick_s"], t["pick_t"])
    operands = (arrived, grad_pre, skip_back, t["y_back"], t["t_back"], t["z_back"])
    field_grad = pl.pallas_call(
        functools.partial(field_grad_kernel, count, own, scale),
        grid=(steps,),
        in_specs=[whole(operands[0]), plane_spec] + [whole(x) for x in operands[2:]],
        out_specs=plane_spec,
        out_shape=plane_shape,
        scratch_shapes=[plane_buf, spec_buf],
        compiler_params=params(),
        name="field_grad",
    )(*operands)
    root = 1.0 / math.sqrt(total)
    square = channels * channels
    skip_grad = stats[0, :square].reshape(channels, channels) * root
    bias_grad = stats[0, square : square + channels] * root
    return (
        output[None],
        field_grad[None],
        spectral_grad.reshape(own * KT, KX, wide),
        skip_grad,
        bias_grad,
    )


def on_any_device(field, cotangent, spectral_weight, skip_weight, bias):
    devices = lax.axis_size("space")
    channels = skip_weight.shape[0]
    fits = (
        field.shape[0] == 1
        and (KY * KZ) % devices == 0
        and devices <= 32
        and field.shape[3] == 2 * KT * channels
        and channels * channels + channels <= field.shape[3]
        and spectral_weight.shape[2] == field.shape[3]
    )
    body = fast_device if fits else on_device
    return body(field, cotangent, spectral_weight, skip_weight, bias)


def solution(mesh):
    in_specs = (
        P(("groups", "space"), None, None, None),
        P(("groups", "space"), None, None, None),
        P("space", None, None),
        P(),
        P(),
    )
    out_specs = (
        P(("groups", "space"), None, None, None),
        P(("groups", "space"), None, None, None),
        P(("groups", "space"), None, None),
        P("groups", None),
        P("groups"),
    )
    return jax.shard_map(
        on_any_device, mesh=mesh, in_specs=in_specs, out_specs=out_specs, check_vma=False
    )
```

```python
import functools
import math

import jax
import jax.numpy as jnp
import ml_dtypes
import numpy as np
from jax import lax
from jax.experimental import pallas as pl
from jax.experimental.pallas import tpu as pltpu
from jax.sharding import PartitionSpec as P

KX = 24
KY = 24
KZ = 24
KT = 8


FULL_PRECISION = lax.Precision.HIGHEST


def angle_pair(freqs, positions, length):
    product = freqs[:, None] * positions[None, :] % length
    angles = product.astype(jnp.float32) * (2.0 * math.pi / length)
    return (jnp.cos(angles), jnp.sin(angles))


def centred(count):
    return jnp.arange(count, dtype=jnp.int32) - count // 2


def kron_eye(base, channels):
    eye_matrix = jnp.eye(channels, dtype=jnp.float32)
    rows_in, cols_in = base.shape
    return (base[:, None, :, None] * eye_matrix[None, :, None, :]).reshape(
        rows_in * channels, cols_in * channels
    )


def block_diagonal(weight, copies):
    eye_matrix = jnp.eye(copies, dtype=jnp.float32)
    width_in, width_out = weight.shape
    return (eye_matrix[:, None, :, None] * weight[None, :, None, :]).reshape(
        copies * width_in, copies * width_out
    )


def turned_forward(values):
    half = values.shape[-1] // 2
    return jnp.concatenate([values[..., half:], -values[..., :half]], axis=-1)


def turned_back(values):
    half = values.shape[-1] // 2
    return jnp.concatenate([-values[..., half:], values[..., :half]], axis=-1)


def plane_spectra(values, time_table, channels):
    cells_x, rows_y, rows_z, _ = values.shape
    mixed_t = jnp.dot(values, time_table, preferred_element_type=jnp.float32)
    cosine_z, sine_z = angle_pair(centred(KZ), jnp.arange(rows_z, dtype=jnp.int32), rows_z)
    table_z = jnp.concatenate([cosine_z, sine_z], axis=1)
    stacked_z = jnp.concatenate([mixed_t, turned_forward(mixed_t)], axis=2)
    along_z = jnp.einsum("kz,xyzm->xykm", table_z, stacked_z, precision=FULL_PRECISION)
    cosine_y, sine_y = angle_pair(centred(KY), jnp.arange(rows_y, dtype=jnp.int32), rows_y)
    table_y = jnp.concatenate([cosine_y, sine_y], axis=1)
    stacked_y = jnp.concatenate([along_z, turned_forward(along_z)], axis=1)
    along_y = jnp.einsum("jy,xykm->xjkm", table_y, stacked_y, precision=FULL_PRECISION)
    grid = along_y.reshape(cells_x, KY, KZ, 2, KT, channels).transpose(0, 1, 2, 4, 3, 5)
    return grid.reshape(cells_x, KY * KZ * KT, 2 * channels)


def plane_fields(planes, inverse_table, rows_y, rows_z):
    cells_x = planes.shape[0]
    channels = planes.shape[2] // 2
    grid = planes.reshape(cells_x, KY, KZ, KT, 2, channels).transpose(0, 1, 2, 4, 3, 5)
    grid = grid.reshape(cells_x, KY, KZ, 2 * KT * channels)
    cosine_y, sine_y = angle_pair(centred(KY), jnp.arange(rows_y, dtype=jnp.int32), rows_y)
    table_y = jnp.concatenate([cosine_y.T, sine_y.T], axis=1)
    stacked_y = jnp.concatenate([grid, turned_back(grid)], axis=1)
    along_y = jnp.einsum("yj,xjkm->xykm", table_y, stacked_y, precision=FULL_PRECISION)
    timed = jnp.dot(
        along_y, inverse_table, precision=FULL_PRECISION, preferred_element_type=jnp.float32
    )
    width_out = timed.shape[3] // 2
    cosine_z, sine_z = angle_pair(centred(KZ), jnp.arange(rows_z, dtype=jnp.int32), rows_z)
    table_z = jnp.stack([cosine_z.T, -sine_z.T], axis=2).reshape(rows_z, 2 * KZ)
    paired = timed.reshape(cells_x, rows_y, 2 * KZ, width_out)
    return jnp.einsum("zk,xykm->xyzm", table_z, paired, precision=FULL_PRECISION)


def along_x(planes, positions, length):
    channels = planes.shape[2] // 2
    cosine_x, sine_x = angle_pair(centred(KX), positions, length)
    real_part = planes[..., :channels]
    imag_part = planes[..., channels:]
    real_k = jnp.einsum("kx,xmc->mkc", cosine_x, real_part, precision=FULL_PRECISION) + jnp.einsum(
        "kx,xmc->mkc", sine_x, imag_part, precision=FULL_PRECISION
    )
    imag_k = jnp.einsum("kx,xmc->mkc", cosine_x, imag_part, precision=FULL_PRECISION) - jnp.einsum(
        "kx,xmc->mkc", sine_x, real_part, precision=FULL_PRECISION
    )
    return jnp.concatenate([real_k, imag_k], axis=2)


def back_along_x(spectra, positions, length):
    channels = spectra.shape[2] // 2
    cosine_x, sine_x = angle_pair(centred(KX), positions, length)
    real_part = spectra[..., :channels]
    imag_part = spectra[..., channels:]
    real_x = jnp.einsum("kx,mkc->xmc", cosine_x, real_part, precision=FULL_PRECISION) - jnp.einsum(
        "kx,mkc->xmc", sine_x, imag_part, precision=FULL_PRECISION
    )
    imag_x = jnp.einsum("kx,mkc->xmc", cosine_x, imag_part, precision=FULL_PRECISION) + jnp.einsum(
        "kx,mkc->xmc", sine_x, real_part, precision=FULL_PRECISION
    )
    return jnp.concatenate([real_x, imag_x], axis=2)


def split_weight(weights, channels):
    modes, freqs, _ = weights.shape
    shaped = weights.reshape(modes, freqs, 2, channels, channels)
    return (shaped[:, :, 0], shaped[:, :, 1])


def mix_forward(spectra, weights):
    channels = spectra.shape[2] // 2
    weight_real, weight_imag = split_weight(weights, channels)
    real_part = spectra[..., :channels]
    imag_part = spectra[..., channels:]
    out_real = jnp.einsum(
        "mki,mkio->mko", real_part, weight_real, precision=FULL_PRECISION
    ) - jnp.einsum("mki,mkio->mko", imag_part, weight_imag, precision=FULL_PRECISION)
    out_imag = jnp.einsum(
        "mki,mkio->mko", real_part, weight_imag, precision=FULL_PRECISION
    ) + jnp.einsum("mki,mkio->mko", imag_part, weight_real, precision=FULL_PRECISION)
    return jnp.concatenate([out_real, out_imag], axis=2)


def mix_adjoint(spectra, weights):
    channels = spectra.shape[2] // 2
    weight_real, weight_imag = split_weight(weights, channels)
    real_part = spectra[..., :channels]
    imag_part = spectra[..., channels:]
    out_real = jnp.einsum(
        "mko,mkio->mki", real_part, weight_real, precision=FULL_PRECISION
    ) + jnp.einsum("mko,mkio->mki", imag_part, weight_imag, precision=FULL_PRECISION)
    out_imag = jnp.einsum(
        "mko,mkio->mki", imag_part, weight_real, precision=FULL_PRECISION
    ) - jnp.einsum("mko,mkio->mki", real_part, weight_imag, precision=FULL_PRECISION)
    return jnp.concatenate([out_real, out_imag], axis=2)


def weight_gradient(source, target):
    modes, freqs, double = source.shape
    channels = double // 2
    src_real = source[..., :channels]
    src_imag = source[..., channels:]
    tgt_real = target[..., :channels]
    tgt_imag = target[..., channels:]
    real_w = jnp.einsum("mki,mko->mkio", src_real, tgt_real, precision=FULL_PRECISION) + jnp.einsum(
        "mki,mko->mkio", src_imag, tgt_imag, precision=FULL_PRECISION
    )
    imag_w = jnp.einsum("mki,mko->mkio", src_real, tgt_imag, precision=FULL_PRECISION) - jnp.einsum(
        "mki,mko->mkio", src_imag, tgt_real, precision=FULL_PRECISION
    )
    return jnp.stack([real_w, imag_w], axis=2).reshape(modes, freqs, 2 * channels * channels)


def gelu_slope(values):
    normal_cdf = 0.5 * (1.0 + jax.scipy.special.erf(values * (1.0 / math.sqrt(2.0))))
    normal_pdf = jnp.exp(-0.5 * values * values) * (1.0 / math.sqrt(2.0 * math.pi))
    return normal_cdf + values * normal_pdf


def on_device(field, cotangent, spectral_weight, skip_weight, bias):
    cells_x, rows_y, rows_z, last_dim = field.shape
    channels = skip_weight.shape[0]
    steps_t = last_dim // channels
    devices = lax.axis_size("space")
    length_x = cells_x * devices
    total = length_x * rows_y * rows_z * steps_t
    every_x = jnp.arange(length_x, dtype=jnp.int32)
    cosine_t, sine_t = angle_pair(
        jnp.arange(KT, dtype=jnp.int32), jnp.arange(steps_t, dtype=jnp.int32), steps_t
    )
    forward_base = jnp.stack([cosine_t.T, -sine_t.T], axis=1).reshape(steps_t, 2 * KT)
    time_table = kron_eye(forward_base, channels).astype(jnp.bfloat16)
    upper_rows = jnp.concatenate([cosine_t, sine_t], axis=1)
    lower_rows = jnp.concatenate([-sine_t, cosine_t], axis=1)
    inverse_base = jnp.concatenate([upper_rows, lower_rows], axis=0) / total
    inverse_table = kron_eye(inverse_base, channels)
    weight_f32 = spectral_weight.astype(jnp.float32)
    skip_f32 = skip_weight.astype(jnp.float32)

    def to_owner(planes):
        arrived = lax.all_to_all(planes, "space", split_axis=1, concat_axis=0, tiled=True)
        return along_x(arrived, every_x, length_x)

    def to_planes(spectra):
        columns = back_along_x(spectra, every_x, length_x)
        return lax.all_to_all(columns, "space", split_axis=0, concat_axis=1, tiled=True)

    own_field = to_owner(plane_spectra(field, time_table, channels))
    skip_table = block_diagonal(skip_f32, steps_t).astype(jnp.bfloat16)
    skip_part = jnp.dot(field, skip_table, preferred_element_type=jnp.float32)
    spectral_part = plane_fields(
        to_planes(mix_forward(own_field, weight_f32)), inverse_table, rows_y, rows_z
    )
    pre_act = spectral_part + skip_part + jnp.tile(bias.astype(jnp.float32), steps_t)
    output = jax.nn.gelu(pre_act, approximate=False).astype(jnp.bfloat16)
    grad_pre = (cotangent.astype(jnp.float32) * gelu_slope(pre_act)).astype(jnp.bfloat16)
    own_grad = to_owner(plane_spectra(grad_pre, time_table, channels))
    skip_back = block_diagonal(skip_f32.T, steps_t).astype(jnp.bfloat16)
    local_back = jnp.dot(grad_pre, skip_back, preferred_element_type=jnp.float32)
    flat_field = field.reshape(-1, last_dim)
    flat_grad = grad_pre.reshape(-1, last_dim)
    outer_sum = lax.dot_general(
        flat_field, flat_grad, (((0,), (0,)), ((), ())), preferred_element_type=jnp.float32
    )
    local_skip = jnp.einsum("tatb->ab", outer_sum.reshape(steps_t, channels, steps_t, channels))
    local_bias = jnp.sum(flat_grad.reshape(-1, steps_t, channels), axis=(0, 1), dtype=jnp.float32)
    skip_total, bias_total = lax.psum((local_skip, local_bias), "space")
    spectral_grad = weight_gradient(own_field, own_grad / total)
    back_part = plane_fields(
        to_planes(mix_adjoint(own_grad, weight_f32)), inverse_table, rows_y, rows_z
    )
    field_grad = (back_part + local_back).astype(jnp.bfloat16)
    scale = 1.0 / math.sqrt(total)
    return (output, field_grad, spectral_grad, skip_total * scale, bias_total * scale)


PAD_ROWS = 8


def split_pair(values):
    high = values.astype(jnp.bfloat16)
    low = (values - high.astype(jnp.float32)).astype(jnp.bfloat16)
    return high, low


def dot32(left, right):
    return jnp.dot(left, right, preferred_element_type=jnp.float32)


def np_angles(freqs, positions, length):
    angles = (np.outer(freqs, positions) % length) * (2.0 * math.pi / length)
    return np.cos(angles), np.sin(angles)


def np_split(table):
    high = table.astype(np.float32).astype(ml_dtypes.bfloat16)
    low = (table - high.astype(np.float64)).astype(np.float32).astype(ml_dtypes.bfloat16)
    return high, low


def np_bf16(table):
    return table.astype(np.float32).astype(ml_dtypes.bfloat16)


def make_tables(rows_y, rows_z, steps_t, channels, devices):
    half = KT * channels
    lanes = 2 * half
    eye_c = np.eye(channels)
    cos_z, sin_z = np_angles(np.arange(KZ) - KZ // 2, np.arange(rows_z), rows_z)
    cos_y, sin_y = np_angles(np.arange(KY) - KY // 2, np.arange(rows_y), rows_y)
    cos_t, sin_t = np_angles(np.arange(KT), np.arange(steps_t), steps_t)
    cos_x, sin_x = np_angles(np.arange(KX) - KX // 2, np.arange(devices), devices)
    tables = {}
    tables["z_fwd"] = np_bf16(np.concatenate([cos_z, sin_z], 0))
    tables["y_fwd"] = np_bf16(np.concatenate([cos_y, sin_y], 0))
    time_fwd = np.kron(np.stack([cos_t.T, -sin_t.T], 1).reshape(steps_t, 2 * KT), eye_c)
    turned = np.concatenate([time_fwd[:, half:], -time_fwd[:, :half]], 1)
    tables["t_fwd"] = np_bf16(np.concatenate([time_fwd, turned], 0))
    y_high, y_low = np_split(np.concatenate([cos_y.T, sin_y.T], 1))
    tables["y_back"] = np.concatenate([y_high, y_high, y_low], 1)
    time_back = np.concatenate(
        [np.concatenate([cos_t, sin_t], 1), np.concatenate([-sin_t, cos_t], 1)], 0
    )
    tables["t_back"] = np_bf16(np.kron(time_back, eye_c))
    tables["z_back"] = np_bf16(np.concatenate([cos_z.T, -sin_z.T], 1))
    eye_p = np.eye(PAD_ROWS)

    def spread(base):
        return np.einsum("kx,pq->pkxq", base, eye_p).reshape(
            PAD_ROWS * KX, devices * PAD_ROWS
        )

    x_high, x_low = np_split(np.concatenate([spread(cos_x), spread(sin_x)], 0))
    tables["x_fwd"] = np.concatenate([x_high, x_high, x_low], 1)
    tables["x_back"] = np.concatenate(
        np_split(np.concatenate([spread(cos_x).T, spread(sin_x).T], 1)), 0
    )
    c = channels
    pick_s = np.zeros((KT, 2, KT, c, 2, 2, c, c))
    pick_t = np.zeros((KT, 2, KT, c, 2, 2, c, c))
    fold_s = np.zeros((KT, 2, 2, c, c, 2, KT, c))
    fold_t = np.zeros((KT, 2, 2, c, c, 2, KT, c))
    for k in range(KT):
        for a in range(c):
            pick_s[k, 0, k, a, 0, :, a, :] = 1
            pick_s[k, 1, k, a, 1, 0, a, :] = 1
            pick_s[k, 1, k, a, 1, 1, a, :] = -1
            pick_t[k, 0, k, a, 0, 0, :, a] = 1
            pick_t[k, 1, k, a, 0, 1, :, a] = 1
            pick_t[k, 1, k, a, 1, 0, :, a] = 1
            pick_t[k, 0, k, a, 1, 1, :, a] = 1
            fold_s[k, 0, 0, :, a, 0, k, a] = 1
            fold_s[k, 1, 1, :, a, 0, k, a] = 1
            fold_s[k, 0, 1, :, a, 1, k, a] = 1
            fold_s[k, 1, 0, :, a, 1, k, a] = 1
            fold_t[k, 0, :, a, :, 0, k, a] = 1
            fold_t[k, 1, 0, a, :, 1, k, a] = 1
            fold_t[k, 1, 1, a, :, 1, k, a] = -1
    wide = 2 * c * c

    def doubled(pick):
        flat = pick.reshape(KT, lanes, 2 * wide)
        return np_bf16(np.concatenate([flat, flat], 1))

    tables["pick_s"] = doubled(pick_s)
    tables["pick_t"] = doubled(pick_t)
    tables["fold_s"] = np_bf16(fold_s.reshape(KT, 2 * wide, lanes))
    tables["fold_t"] = np_bf16(fold_t.reshape(KT, 2 * wide, lanes))
    return {name: jnp.asarray(table) for name, table in tables.items()}


def half_sign(shape, first, second):
    lane = lax.broadcasted_iota(jnp.int32, shape, 1)
    return jnp.where(lane < shape[1] // 2, first, second).astype(jnp.float32)


def roll_half(values):
    return pltpu.roll(values, values.shape[1] // 2, 1)


def z_forward(rows, count, z_table, t_table):
    pieces = []
    for y in range(count):
        both = dot32(z_table, rows(y))
        pieces.append(jnp.concatenate([both[:KZ], both[KZ:]], axis=1))
    stacked = jnp.concatenate(pieces, axis=0).astype(jnp.bfloat16)
    return dot32(stacked, t_table)


def y_forward(zbuf, spec, y_table, rows_y, lanes):
    sign = half_sign((KY, lanes), 1.0, -1.0)
    for kz in range(KZ):
        column = zbuf[pl.ds(kz, rows_y, stride=KZ), :].astype(jnp.bfloat16)
        both = dot32(y_table, column)
        spec[pl.ds(kz, KY, stride=KZ), :] = both[:KY] + sign * roll_half(both[KY:])


def y_backward(spec, ubuf, y_table, rows_y, lanes):
    sign = half_sign((KY, lanes), -1.0, 1.0)
    for kz in range(KZ):
        column = spec[pl.ds(kz, KY, stride=KZ), :]
        both = jnp.concatenate([column, sign * roll_half(column)], axis=0)
        high, low = split_pair(both)
        stacked = jnp.concatenate([high, low, high], axis=0)
        ubuf[pl.ds(kz, rows_y, stride=KZ), :] = dot32(y_table, stacked)


def z_backward(ubuf, start, count, t_table):
    lanes = ubuf.shape[1]
    rows = ubuf[pl.ds(start, count * KZ), :].astype(jnp.bfloat16)
    timed = dot32(rows, t_table)
    pieces = []
    for y in range(count):
        mine = timed[y * KZ : (y + 1) * KZ]
        pieces.append(
            jnp.concatenate([mine[:, :lanes], mine[:, lanes:]], axis=0).astype(jnp.bfloat16)
        )
    return pieces


def write_blocks(spec, out_ref, own, stats):
    devices, padded, lanes = out_ref.shape
    spare = padded - own
    if spare > 1:
        zeros = jnp.zeros((spare - 1, lanes), jnp.float32)
        tail = jnp.concatenate([stats, zeros], axis=0)
    else:
        tail = stats
    for d in range(devices):
        out_ref[d, 0:own, :] = spec[d * own : (d + 1) * own, :]
        out_ref[d, own:padded, :] = tail


def read_blocks(in_ref, spec, own, scale):
    for d in range(in_ref.shape[0]):
        spec[d * own : (d + 1) * own, :] = in_ref[d, 0:own, :] * scale


def greet_all():
    devices = lax.axis_size("space")
    me = lax.axis_index("space")
    barrier = pltpu.get_barrier_semaphore()

    def signal(offset, carry):
        peer = lax.rem(me + offset, devices)
        pl.semaphore_signal(
            barrier, inc=1, device_id={"space": peer}, device_id_type=pl.DeviceIdType.MESH
        )
        return carry

    lax.fori_loop(1, devices, signal, 0)


def await_all():
    pl.semaphore_wait(pltpu.get_barrier_semaphore(), lax.axis_size("space") - 1)


def peer_copy(offset, part, rows, send, recv, send_sems, recv_sems):
    devices = lax.axis_size("space")
    me = lax.axis_index("space")
    peer = lax.rem(me + offset, devices)
    low, high = rows
    return pltpu.make_async_remote_copy(
        src_ref=send.at[peer, low:high],
        dst_ref=recv.at[me, low:high],
        send_sem=send_sems.at[part, offset],
        recv_sem=recv_sems.at[part, offset],
        device_id={"space": peer},
        device_id_type=pl.DeviceIdType.MESH,
    )


def each_peer(action, part, rows, buffers):
    def body(offset, carry):
        action(peer_copy(offset, part, rows, *buffers))
        return carry

    lax.fori_loop(1, lax.axis_size("space"), body, 0)


def start_part(part, rows, buffers):
    each_peer(lambda copy: copy.start(), part, rows, buffers)
    send, recv = buffers[:2]
    me = lax.axis_index("space")
    low, high = rows
    recv[me, low:high, :] = send[me, low:high, :]


def row_parts(padded):
    tiles = padded // PAD_ROWS
    cut = max(tiles * 2 // 5, 1)
    parts = [(0, cut), (cut, tiles)] if cut < tiles else [(0, tiles)]
    return parts


def exchange_and_mix(to_owner, to_planes, mix_tile, out_ref):
    padded = to_owner[0].shape[1]
    parts = row_parts(padded)
    rows = [(low * PAD_ROWS, high * PAD_ROWS) for low, high in parts]
    for part in range(len(parts)):
        start_part(part, rows[part], to_owner)
    for part, (low, high) in enumerate(parts):
        each_peer(lambda copy: copy.wait_recv(), part, rows[part], to_owner)
        for tile in range(low, high):
            mix_tile(tile)
        start_part(part, rows[part], to_planes)
    for part in range(len(parts)):
        each_peer(lambda copy: copy.wait_recv(), part, rows[part], to_planes)
    for part in range(len(parts)):
        each_peer(lambda copy: copy.wait_send(), part, rows[part], to_owner)
        each_peer(lambda copy: copy.wait_send(), part, rows[part], to_planes)
    out_ref[...] = to_planes[1][...]


def mix_one_tile(tile, in_ref, w_ref, tables, spectrum_ref, send_ref):
    xf_ref, xb_ref, pick_ref, fold_ref = tables
    own = w_ref.shape[0]
    rows = PAD_ROWS * KX
    first = tile * PAD_ROWS
    pairs = min(PAD_ROWS, own - first)
    if pairs <= 0:
        send_ref[:, first : first + PAD_ROWS, :] = jnp.zeros(
            (send_ref.shape[0], PAD_ROWS, send_ref.shape[2]), jnp.float32
        )
        return
    spectrum = x_forward(in_ref, tile, xf_ref[...])
    spectrum_ref[tile * rows : (tile + 1) * rows, :] = spectrum
    mixed = mixed_rows(spectrum[: pairs * KX], w_ref, first, pairs, pick_ref, fold_ref)
    x_backward(mixed, send_ref, tile, xb_ref[...])


def repeat_matrix(lanes, channels):
    row = lax.broadcasted_iota(jnp.int32, (lanes, channels), 0)
    column = lax.broadcasted_iota(jnp.int32, (lanes, channels), 1)
    return (row % channels == column).astype(jnp.float32).astype(jnp.bfloat16)


def repeated_table(weight, lanes, flip):
    channels = weight.shape[0]
    repeat = repeat_matrix(lanes, channels)
    inner = lax.dot_general(
        repeat,
        weight,
        (((1,), (1 if flip else 0,)), ((), ())),
        preferred_element_type=jnp.float32,
    ).astype(jnp.bfloat16)
    full = lax.dot_general(
        inner, repeat, (((1,), (1,)), ((), ())), preferred_element_type=jnp.float32
    )
    row = lax.broadcasted_iota(jnp.int32, (lanes, lanes), 0)
    lane = lax.broadcasted_iota(jnp.int32, (lanes, lanes), 1)
    return jnp.where(row // channels == lane // channels, full, 0.0).astype(jnp.bfloat16)


def spectrum_kernel(
    count,
    own,
    f_ref,
    zt_ref,
    tt_ref,
    yt_ref,
    w_ref,
    xf_ref,
    xb_ref,
    pick_ref,
    fold_ref,
    spectrum_ref,
    out_ref,
    zbuf,
    spec,
    send_a,
    recv_a,
    send_b,
    recv_b,
    send_sems_a,
    recv_sems_a,
    send_sems_b,
    recv_sems_b,
):
    step = pl.program_id(0)

    @pl.when(step == 0)
    def _():
        greet_all()

    lanes = zbuf.shape[1]
    chunk = z_forward(lambda y: f_ref[y], count, zt_ref[...], tt_ref[...])
    zbuf[pl.ds(pl.multiple_of(step * (count * KZ), 8), count * KZ), :] = chunk

    @pl.when(step == pl.num_programs(0) - 1)
    def _():
        y_forward(zbuf, spec, yt_ref[...], zbuf.shape[0] // KZ, lanes)
        write_blocks(spec, send_a, own, jnp.zeros((1, lanes), jnp.float32))
        await_all()
        tables = (xf_ref, xb_ref, pick_ref, fold_ref)
        exchange_and_mix(
            (send_a, recv_a, send_sems_a, recv_sems_a),
            (send_b, recv_b, send_sems_b, recv_sems_b),
            lambda tile: mix_one_tile(tile, recv_a, w_ref, tables, spectrum_ref, send_b),
            out_ref,
        )


def activation_kernel(
    count,
    own,
    scale,
    channels,
    in_ref,
    f_ref,
    cot_ref,
    skip_ref,
    bias_ref,
    yb_ref,
    tb_ref,
    zb_ref,
    zt_ref,
    tt_ref,
    yt_ref,
    w_ref,
    xf_ref,
    xb_ref,
    pick_ref,
    fold_ref,
    out_ref,
    grad_ref,
    spectrum_ref,
    arrived_ref,
    stats_ref,
    ubuf,
    zbuf,
    spec,
    outer,
    total_row,
    skip_table,
    bias_buf,
    send_a,
    recv_a,
    send_b,
    recv_b,
    send_sems_a,
    recv_sems_a,
    send_sems_b,
    recv_sems_b,
):
    step = pl.program_id(0)
    lanes = ubuf.shape[1]
    rows_y = ubuf.shape[0] // KZ

    @pl.when(step == 0)
    def _():
        greet_all()
        skip_table[...] = repeated_table(skip_ref[...], lanes, False)
        bias_buf[...] = lax.dot_general(
            bias_ref[...],
            repeat_matrix(lanes, channels),
            (((1,), (1,)), ((), ())),
            preferred_element_type=jnp.float32,
        )
        read_blocks(in_ref, spec, own, scale)
        y_backward(spec, ubuf, yb_ref[...], rows_y, lanes)
        outer[...] = jnp.zeros_like(outer)
        total_row[...] = jnp.zeros_like(total_row)

    start = pl.multiple_of(step * (count * KZ), 8)
    pieces = z_backward(ubuf, start, count, tb_ref[...])
    bias_row = bias_buf[...]
    for y in range(count):
        field = f_ref[y]
        pre = dot32(zb_ref[...], pieces[y]) + dot32(field, skip_table[...]) + bias_row
        cdf = 0.5 * (1.0 + lax.erf(pre * (1.0 / math.sqrt(2.0))))
        pdf = jnp.exp(-0.5 * pre * pre) * (1.0 / math.sqrt(2.0 * math.pi))
        out_ref[y] = (pre * cdf).astype(jnp.bfloat16)
        slope = cdf + pre * pdf
        grad = (cot_ref[y].astype(jnp.float32) * slope).astype(jnp.bfloat16)
        grad_ref[y] = grad
        total_row[...] += jnp.sum(
            grad.astype(jnp.float32).reshape(-1, 8, lanes), axis=0
        )
    flat_f = f_ref[...].reshape(-1, lanes)
    flat_g = grad_ref[...].reshape(-1, lanes)
    outer[...] += lax.dot_general(
        flat_f, flat_g, (((0,), (0,)), ((), ())), preferred_element_type=jnp.float32
    )
    chunk = z_forward(lambda y: grad_ref[y], count, zt_ref[...], tt_ref[...])
    zbuf[pl.ds(start, count * KZ), :] = chunk

    @pl.when(step == pl.num_programs(0) - 1)
    def _():
        y_forward(zbuf, spec, yt_ref[...], rows_y, lanes)
        row = lax.broadcasted_iota(jnp.int32, (lanes, lanes), 0)
        lane = lax.broadcasted_iota(jnp.int32, (lanes, lanes), 1)
        same_t = row // channels == lane // channels
        same_c = (row % channels == lane % channels).astype(jnp.float32)
        diagonal = jnp.where(same_t, outer[...], 0.0)
        per_c = jnp.dot(diagonal, same_c, precision=FULL_PRECISION)
        keep = (row % channels) == (lane // channels)
        skip_row = jnp.sum(jnp.where(keep, per_c, 0.0), axis=0, keepdims=True)
        folded = jnp.dot(total_row[...], same_c, precision=FULL_PRECISION)
        group = lax.broadcasted_iota(jnp.int32, (1, lanes), 1) // channels
        bias_sum = jnp.sum(folded, axis=0, keepdims=True)
        bias_sum = jnp.where(group == channels, bias_sum, 0.0)
        write_blocks(spec, send_a, own, skip_row + bias_sum)
        await_all()
        tables = (xf_ref, xb_ref, pick_ref, fold_ref)
        exchange_and_mix(
            (send_a, recv_a, send_sems_a, recv_sems_a),
            (send_b, recv_b, send_sems_b, recv_sems_b),
            lambda tile: mix_one_tile(tile, recv_a, w_ref, tables, spectrum_ref, send_b),
            arrived_ref,
        )
        stats_ref[...] = jnp.sum(recv_a[:, own, :], axis=0, keepdims=True)


def field_grad_kernel(
    count,
    own,
    scale,
    root,
    in_ref,
    grad_ref,
    skip_ref,
    stats_ref,
    yb_ref,
    tb_ref,
    zb_ref,
    out_ref,
    skip_out,
    bias_out,
    ubuf,
    spec,
    skip_table,
):
    step = pl.program_id(0)
    lanes = ubuf.shape[1]

    @pl.when(step == 0)
    def _():
        read_blocks(in_ref, spec, own, scale)
        y_backward(spec, ubuf, yb_ref[...], ubuf.shape[0] // KZ, lanes)
        skip_table[...] = repeated_table(skip_ref[...], lanes, True)
        channels = skip_ref.shape[0]
        group = lax.broadcasted_iota(jnp.int32, (2 * channels, lanes), 1) // channels
        row = lax.broadcasted_iota(jnp.int32, (2 * channels, lanes), 0)
        chosen = jnp.where(group == row, stats_ref[...] * root, 0.0)
        fold = repeat_matrix(lanes, channels).astype(jnp.float32)
        folded = jnp.dot(chosen, fold, precision=FULL_PRECISION)
        skip_out[...] = folded[:channels]
        bias_out[...] = folded[channels : channels + 1]

    start = pl.multiple_of(step * (count * KZ), 8)
    pieces = z_backward(ubuf, start, count, tb_ref[...])
    for y in range(count):
        value = dot32(zb_ref[...], pieces[y]) + dot32(grad_ref[y], skip_table[...])
        out_ref[y] = value.astype(jnp.bfloat16)


def x_forward(in_ref, tile, x_table):
    devices, _, lanes = in_ref.shape
    block = in_ref[:, tile * PAD_ROWS : (tile + 1) * PAD_ROWS, :]
    block = block.reshape(devices * PAD_ROWS, lanes)
    high, low = split_pair(block)
    both = dot32(x_table, jnp.concatenate([high, low, high], axis=0))
    rows = PAD_ROWS * KX
    return both[:rows] + half_sign((rows, lanes), 1.0, -1.0) * roll_half(both[rows:])


def x_backward(columns, out_ref, tile, x_table):
    devices, _, lanes = out_ref.shape
    missing = PAD_ROWS * KX - columns.shape[0]
    if missing:
        columns = jnp.concatenate([columns, jnp.zeros((missing, lanes), jnp.float32)], axis=0)
    turned = half_sign(columns.shape, -1.0, 1.0) * roll_half(columns)
    high, low = split_pair(jnp.concatenate([columns, turned], axis=0))
    size = devices * PAD_ROWS
    from_high = dot32(x_table, high)
    rows = from_high[:size] + from_high[size:] + dot32(x_table[:size], low)
    out_ref[:, tile * PAD_ROWS : (tile + 1) * PAD_ROWS, :] = rows.reshape(
        devices, PAD_ROWS, lanes
    )


def mixed_rows(spectrum, w_ref, first, pairs, pick_ref, fold_ref):
    wide = w_ref.shape[3]
    high, low = split_pair(spectrum)
    doubled = jnp.concatenate([high, low], axis=1)
    total = None
    for k in range(KT):
        terms = dot32(doubled, pick_ref[k])
        weight = w_ref[first : first + pairs, k].astype(jnp.float32).reshape(pairs * KX, wide)
        product = jnp.concatenate([terms[:, :wide] * weight, terms[:, wide:] * weight], axis=1)
        part = dot32(product.astype(jnp.bfloat16), fold_ref[k])
        total = part if total is None else total + part
    return total


def weight_gradient_kernel(scale, s_ref, t_ref, ps_ref, pt_ref, out_ref):
    pairs, _, _, wide = out_ref.shape
    for_s = jnp.concatenate(split_pair(s_ref[...]), axis=1)
    for_t = jnp.concatenate(split_pair(t_ref[...] * scale), axis=1)
    for k in range(KT):
        left = dot32(for_s, ps_ref[k])
        right = dot32(for_t, pt_ref[k])
        value = left[:, :wide] * right[:, :wide] + left[:, wide:] * right[:, wide:]
        out_ref[:, k] = value.reshape(pairs, KX, wide)


def whole(array):
    zeros = (0,) * len(array.shape)
    return pl.BlockSpec(array.shape, lambda *_: zeros)


def params(**extra):
    return pltpu.CompilerParams(vmem_limit_bytes=48 * 1024 * 1024, **extra)


def fast_device(field, cotangent, spectral_weight, skip_weight, bias):
    _, rows_y, rows_z, lanes = field.shape
    channels = skip_weight.shape[0]
    steps_t = lanes // channels
    devices = lax.axis_size("space")
    total = devices * rows_y * rows_z * steps_t
    scale = 1.0 / total
    own = KY * KZ // devices
    padded = (own // PAD_ROWS + 1) * PAD_ROWS
    wide = spectral_weight.shape[2]
    t = make_tables(rows_y, rows_z, steps_t, channels, devices)
    count = 16
    while rows_y % count:
        count //= 2
    steps = rows_y // count
    field = field.reshape(rows_y, rows_z, lanes)
    cotangent = cotangent.reshape(rows_y, rows_z, lanes)
    weights = spectral_weight.reshape(own, KT, KX, wide)
    bias_row = bias.reshape(1, channels)
    plane_spec = pl.BlockSpec((count, rows_z, lanes), lambda i: (i, 0, 0))
    plane_shape = jax.ShapeDtypeStruct((rows_y, rows_z, lanes), jnp.bfloat16)
    block_shape = jax.ShapeDtypeStruct((devices, padded, lanes), jnp.float32)
    block_spec = pl.BlockSpec((devices, padded, lanes), lambda *_: (0, 0, 0))
    mode_rows = pl.cdiv(own, PAD_ROWS) * PAD_ROWS * KX
    spectrum_shape = jax.ShapeDtypeStruct((mode_rows, lanes), jnp.float32)
    plane_buf = pltpu.VMEM((rows_y * KZ, lanes), jnp.float32)
    spec_buf = pltpu.VMEM((KY * KZ, lanes), jnp.float32)

    parts = len(row_parts(padded))
    block_buf = pltpu.VMEM((devices, padded, lanes), jnp.float32)
    sems = pltpu.SemaphoreType.DMA((parts, devices))
    link_scratch = [block_buf] * 4 + [sems] * 4
    spectrum_spec = pl.BlockSpec(spectrum_shape.shape, lambda *_: (0, 0))
    mixing_s = (weights, t["x_fwd"], t["x_back"], t["pick_s"], t["fold_s"])
    mixing_t = (weights, t["x_fwd"], t["x_back"], t["pick_t"], t["fold_t"])
    operands = (field, t["z_fwd"], t["t_fwd"], t["y_fwd"]) + mixing_s
    own_field, arrived = pl.pallas_call(
        functools.partial(spectrum_kernel, count, own),
        grid=(steps,),
        in_specs=[plane_spec] + [whole(x) for x in operands[1:]],
        out_specs=[spectrum_spec, block_spec],
        out_shape=[spectrum_shape, block_shape],
        scratch_shapes=[plane_buf, spec_buf] + link_scratch,
        compiler_params=params(collective_id=0, has_side_effects=True),
        name="forward_mix",
    )(*operands)
    operands = (
        arrived,
        field,
        cotangent,
        skip_weight,
        bias_row,
        t["y_back"],
        t["t_back"],
        t["z_back"],
        t["z_fwd"],
        t["t_fwd"],
        t["y_fwd"],
    ) + mixing_t
    stats_shape = jax.ShapeDtypeStruct((1, lanes), jnp.float32)
    output, grad_pre, own_grad, arrived, stats = pl.pallas_call(
        functools.partial(activation_kernel, count, own, scale, channels),
        grid=(steps,),
        in_specs=[whole(operands[0]), plane_spec, plane_spec] + [whole(x) for x in operands[3:]],
        out_specs=[plane_spec, plane_spec, spectrum_spec, block_spec, whole(stats_shape)],
        out_shape=[plane_shape, plane_shape, spectrum_shape, block_shape, stats_shape],
        scratch_shapes=[
            plane_buf,
            plane_buf,
            spec_buf,
            pltpu.VMEM((lanes, lanes), jnp.float32),
            pltpu.VMEM((8, lanes), jnp.float32),
            pltpu.VMEM((lanes, lanes), jnp.bfloat16),
            pltpu.VMEM((1, lanes), jnp.float32),
        ]
        + link_scratch,
        compiler_params=params(collective_id=1, has_side_effects=True),
        name="activation_mix",
    )(*operands)
    pairs = 4 if own % 4 == 0 else 1
    mode_spec = pl.BlockSpec((pairs * KX, lanes), lambda i: (i, 0))
    spectral_grad = pl.pallas_call(
        functools.partial(weight_gradient_kernel, scale),
        grid=(own // pairs,),
        in_specs=[mode_spec, mode_spec, whole(t["pick_s"]), whole(t["pick_t"])],
        out_specs=pl.BlockSpec((pairs, KT, KX, wide), lambda i: (i, 0, 0, 0)),
        out_shape=jax.ShapeDtypeStruct((own, KT, KX, wide), jnp.float32),
        compiler_params=params(),
        cost_estimate=pl.CostEstimate(
            flops=4 * own * KX * KT * 65536, bytes_accessed=8 * own * KX * KT * wide, transcendentals=0
        ),
        name="weight_gradient",
    )(own_field, own_grad, t["pick_s"], t["pick_t"])
    operands = (arrived, grad_pre, skip_weight, stats, t["y_back"], t["t_back"], t["z_back"])
    root = 1.0 / math.sqrt(total)
    square_shape = jax.ShapeDtypeStruct((channels, channels), jnp.float32)
    line_shape = jax.ShapeDtypeStruct((1, channels), jnp.float32)
    field_grad, skip_grad, bias_grad = pl.pallas_call(
        functools.partial(field_grad_kernel, count, own, scale, root),
        grid=(steps,),
        in_specs=[whole(operands[0]), plane_spec] + [whole(x) for x in operands[2:]],
        out_specs=[plane_spec, whole(square_shape), whole(line_shape)],
        out_shape=[plane_shape, square_shape, line_shape],
        scratch_shapes=[plane_buf, spec_buf, pltpu.VMEM((lanes, lanes), jnp.bfloat16)],
        compiler_params=params(),
        name="field_grad",
    )(*operands)
    return (
        output[None],
        field_grad[None],
        spectral_grad.reshape(own * KT, KX, wide),
        skip_grad,
        bias_grad.reshape(channels),
    )


def on_any_device(field, cotangent, spectral_weight, skip_weight, bias):
    devices = lax.axis_size("space")
    channels = skip_weight.shape[0]
    fits = (
        field.shape[0] == 1
        and (KY * KZ) % devices == 0
        and devices <= 32
        and field.shape[3] == 2 * KT * channels
        and channels * channels + channels <= field.shape[3]
        and spectral_weight.shape[2] == field.shape[3]
    )
    body = fast_device if fits else on_device
    return body(field, cotangent, spectral_weight, skip_weight, bias)


def solution(mesh):
    in_specs = (
        P(("groups", "space"), None, None, None),
        P(("groups", "space"), None, None, None),
        P("space", None, None),
        P(),
        P(),
    )
    out_specs = (
        P(("groups", "space"), None, None, None),
        P(("groups", "space"), None, None, None),
        P(("groups", "space"), None, None),
        P("groups", None),
        P("groups"),
    )
    return jax.shard_map(
        on_any_device, mesh=mesh, in_specs=in_specs, out_specs=out_specs, check_vma=False
    )
```

```python
import functools
import math

import jax
import jax.numpy as jnp
import ml_dtypes
import numpy as np
from jax import lax
from jax.experimental import pallas as pl
from jax.experimental.pallas import tpu as pltpu
from jax.sharding import PartitionSpec as P

KX = 24
KY = 24
KZ = 24
KT = 8


FULL_PRECISION = lax.Precision.HIGHEST


def angle_pair(freqs, positions, length):
    product = freqs[:, None] * positions[None, :] % length
    angles = product.astype(jnp.float32) * (2.0 * math.pi / length)
    return (jnp.cos(angles), jnp.sin(angles))


def centred(count):
    return jnp.arange(count, dtype=jnp.int32) - count // 2


def kron_eye(base, channels):
    eye_matrix = jnp.eye(channels, dtype=jnp.float32)
    rows_in, cols_in = base.shape
    return (base[:, None, :, None] * eye_matrix[None, :, None, :]).reshape(
        rows_in * channels, cols_in * channels
    )


def block_diagonal(weight, copies):
    eye_matrix = jnp.eye(copies, dtype=jnp.float32)
    width_in, width_out = weight.shape
    return (eye_matrix[:, None, :, None] * weight[None, :, None, :]).reshape(
        copies * width_in, copies * width_out
    )


def turned_forward(values):
    half = values.shape[-1] // 2
    return jnp.concatenate([values[..., half:], -values[..., :half]], axis=-1)


def turned_back(values):
    half = values.shape[-1] // 2
    return jnp.concatenate([-values[..., half:], values[..., :half]], axis=-1)


def plane_spectra(values, time_table, channels):
    cells_x, rows_y, rows_z, _ = values.shape
    mixed_t = jnp.dot(values, time_table, preferred_element_type=jnp.float32)
    cosine_z, sine_z = angle_pair(centred(KZ), jnp.arange(rows_z, dtype=jnp.int32), rows_z)
    table_z = jnp.concatenate([cosine_z, sine_z], axis=1)
    stacked_z = jnp.concatenate([mixed_t, turned_forward(mixed_t)], axis=2)
    along_z = jnp.einsum("kz,xyzm->xykm", table_z, stacked_z, precision=FULL_PRECISION)
    cosine_y, sine_y = angle_pair(centred(KY), jnp.arange(rows_y, dtype=jnp.int32), rows_y)
    table_y = jnp.concatenate([cosine_y, sine_y], axis=1)
    stacked_y = jnp.concatenate([along_z, turned_forward(along_z)], axis=1)
    along_y = jnp.einsum("jy,xykm->xjkm", table_y, stacked_y, precision=FULL_PRECISION)
    grid = along_y.reshape(cells_x, KY, KZ, 2, KT, channels).transpose(0, 1, 2, 4, 3, 5)
    return grid.reshape(cells_x, KY * KZ * KT, 2 * channels)


def plane_fields(planes, inverse_table, rows_y, rows_z):
    cells_x = planes.shape[0]
    channels = planes.shape[2] // 2
    grid = planes.reshape(cells_x, KY, KZ, KT, 2, channels).transpose(0, 1, 2, 4, 3, 5)
    grid = grid.reshape(cells_x, KY, KZ, 2 * KT * channels)
    cosine_y, sine_y = angle_pair(centred(KY), jnp.arange(rows_y, dtype=jnp.int32), rows_y)
    table_y = jnp.concatenate([cosine_y.T, sine_y.T], axis=1)
    stacked_y = jnp.concatenate([grid, turned_back(grid)], axis=1)
    along_y = jnp.einsum("yj,xjkm->xykm", table_y, stacked_y, precision=FULL_PRECISION)
    timed = jnp.dot(
        along_y, inverse_table, precision=FULL_PRECISION, preferred_element_type=jnp.float32
    )
    width_out = timed.shape[3] // 2
    cosine_z, sine_z = angle_pair(centred(KZ), jnp.arange(rows_z, dtype=jnp.int32), rows_z)
    table_z = jnp.stack([cosine_z.T, -sine_z.T], axis=2).reshape(rows_z, 2 * KZ)
    paired = timed.reshape(cells_x, rows_y, 2 * KZ, width_out)
    return jnp.einsum("zk,xykm->xyzm", table_z, paired, precision=FULL_PRECISION)


def along_x(planes, positions, length):
    channels = planes.shape[2] // 2
    cosine_x, sine_x = angle_pair(centred(KX), positions, length)
    real_part = planes[..., :channels]
    imag_part = planes[..., channels:]
    real_k = jnp.einsum("kx,xmc->mkc", cosine_x, real_part, precision=FULL_PRECISION) + jnp.einsum(
        "kx,xmc->mkc", sine_x, imag_part, precision=FULL_PRECISION
    )
    imag_k = jnp.einsum("kx,xmc->mkc", cosine_x, imag_part, precision=FULL_PRECISION) - jnp.einsum(
        "kx,xmc->mkc", sine_x, real_part, precision=FULL_PRECISION
    )
    return jnp.concatenate([real_k, imag_k], axis=2)


def back_along_x(spectra, positions, length):
    channels = spectra.shape[2] // 2
    cosine_x, sine_x = angle_pair(centred(KX), positions, length)
    real_part = spectra[..., :channels]
    imag_part = spectra[..., channels:]
    real_x = jnp.einsum("kx,mkc->xmc", cosine_x, real_part, precision=FULL_PRECISION) - jnp.einsum(
        "kx,mkc->xmc", sine_x, imag_part, precision=FULL_PRECISION
    )
    imag_x = jnp.einsum("kx,mkc->xmc", cosine_x, imag_part, precision=FULL_PRECISION) + jnp.einsum(
        "kx,mkc->xmc", sine_x, real_part, precision=FULL_PRECISION
    )
    return jnp.concatenate([real_x, imag_x], axis=2)


def split_weight(weights, channels):
    modes, freqs, _ = weights.shape
    shaped = weights.reshape(modes, freqs, 2, channels, channels)
    return (shaped[:, :, 0], shaped[:, :, 1])


def mix_forward(spectra, weights):
    channels = spectra.shape[2] // 2
    weight_real, weight_imag = split_weight(weights, channels)
    real_part = spectra[..., :channels]
    imag_part = spectra[..., channels:]
    out_real = jnp.einsum(
        "mki,mkio->mko", real_part, weight_real, precision=FULL_PRECISION
    ) - jnp.einsum("mki,mkio->mko", imag_part, weight_imag, precision=FULL_PRECISION)
    out_imag = jnp.einsum(
        "mki,mkio->mko", real_part, weight_imag, precision=FULL_PRECISION
    ) + jnp.einsum("mki,mkio->mko", imag_part, weight_real, precision=FULL_PRECISION)
    return jnp.concatenate([out_real, out_imag], axis=2)


def mix_adjoint(spectra, weights):
    channels = spectra.shape[2] // 2
    weight_real, weight_imag = split_weight(weights, channels)
    real_part = spectra[..., :channels]
    imag_part = spectra[..., channels:]
    out_real = jnp.einsum(
        "mko,mkio->mki", real_part, weight_real, precision=FULL_PRECISION
    ) + jnp.einsum("mko,mkio->mki", imag_part, weight_imag, precision=FULL_PRECISION)
    out_imag = jnp.einsum(
        "mko,mkio->mki", imag_part, weight_real, precision=FULL_PRECISION
    ) - jnp.einsum("mko,mkio->mki", real_part, weight_imag, precision=FULL_PRECISION)
    return jnp.concatenate([out_real, out_imag], axis=2)


def weight_gradient(source, target):
    modes, freqs, double = source.shape
    channels = double // 2
    src_real = source[..., :channels]
    src_imag = source[..., channels:]
    tgt_real = target[..., :channels]
    tgt_imag = target[..., channels:]
    real_w = jnp.einsum("mki,mko->mkio", src_real, tgt_real, precision=FULL_PRECISION) + jnp.einsum(
        "mki,mko->mkio", src_imag, tgt_imag, precision=FULL_PRECISION
    )
    imag_w = jnp.einsum("mki,mko->mkio", src_real, tgt_imag, precision=FULL_PRECISION) - jnp.einsum(
        "mki,mko->mkio", src_imag, tgt_real, precision=FULL_PRECISION
    )
    return jnp.stack([real_w, imag_w], axis=2).reshape(modes, freqs, 2 * channels * channels)


def gelu_slope(values):
    normal_cdf = 0.5 * (1.0 + jax.scipy.special.erf(values * (1.0 / math.sqrt(2.0))))
    normal_pdf = jnp.exp(-0.5 * values * values) * (1.0 / math.sqrt(2.0 * math.pi))
    return normal_cdf + values * normal_pdf


def on_device(field, cotangent, spectral_weight, skip_weight, bias):
    cells_x, rows_y, rows_z, last_dim = field.shape
    channels = skip_weight.shape[0]
    steps_t = last_dim // channels
    devices = lax.axis_size("space")
    length_x = cells_x * devices
    total = length_x * rows_y * rows_z * steps_t
    every_x = jnp.arange(length_x, dtype=jnp.int32)
    cosine_t, sine_t = angle_pair(
        jnp.arange(KT, dtype=jnp.int32), jnp.arange(steps_t, dtype=jnp.int32), steps_t
    )
    forward_base = jnp.stack([cosine_t.T, -sine_t.T], axis=1).reshape(steps_t, 2 * KT)
    time_table = kron_eye(forward_base, channels).astype(jnp.bfloat16)
    upper_rows = jnp.concatenate([cosine_t, sine_t], axis=1)
    lower_rows = jnp.concatenate([-sine_t, cosine_t], axis=1)
    inverse_base = jnp.concatenate([upper_rows, lower_rows], axis=0) / total
    inverse_table = kron_eye(inverse_base, channels)
    weight_f32 = spectral_weight.astype(jnp.float32)
    skip_f32 = skip_weight.astype(jnp.float32)

    def to_owner(planes):
        arrived = lax.all_to_all(planes, "space", split_axis=1, concat_axis=0, tiled=True)
        return along_x(arrived, every_x, length_x)

    def to_planes(spectra):
        columns = back_along_x(spectra, every_x, length_x)
        return lax.all_to_all(columns, "space", split_axis=0, concat_axis=1, tiled=True)

    own_field = to_owner(plane_spectra(field, time_table, channels))
    skip_table = block_diagonal(skip_f32, steps_t).astype(jnp.bfloat16)
    skip_part = jnp.dot(field, skip_table, preferred_element_type=jnp.float32)
    spectral_part = plane_fields(
        to_planes(mix_forward(own_field, weight_f32)), inverse_table, rows_y, rows_z
    )
    pre_act = spectral_part + skip_part + jnp.tile(bias.astype(jnp.float32), steps_t)
    output = jax.nn.gelu(pre_act, approximate=False).astype(jnp.bfloat16)
    grad_pre = (cotangent.astype(jnp.float32) * gelu_slope(pre_act)).astype(jnp.bfloat16)
    own_grad = to_owner(plane_spectra(grad_pre, time_table, channels))
    skip_back = block_diagonal(skip_f32.T, steps_t).astype(jnp.bfloat16)
    local_back = jnp.dot(grad_pre, skip_back, preferred_element_type=jnp.float32)
    flat_field = field.reshape(-1, last_dim)
    flat_grad = grad_pre.reshape(-1, last_dim)
    outer_sum = lax.dot_general(
        flat_field, flat_grad, (((0,), (0,)), ((), ())), preferred_element_type=jnp.float32
    )
    local_skip = jnp.einsum("tatb->ab", outer_sum.reshape(steps_t, channels, steps_t, channels))
    local_bias = jnp.sum(flat_grad.reshape(-1, steps_t, channels), axis=(0, 1), dtype=jnp.float32)
    skip_total, bias_total = lax.psum((local_skip, local_bias), "space")
    spectral_grad = weight_gradient(own_field, own_grad / total)
    back_part = plane_fields(
        to_planes(mix_adjoint(own_grad, weight_f32)), inverse_table, rows_y, rows_z
    )
    field_grad = (back_part + local_back).astype(jnp.bfloat16)
    scale = 1.0 / math.sqrt(total)
    return (output, field_grad, spectral_grad, skip_total * scale, bias_total * scale)


PAD_ROWS = 8


def split_pair(values):
    high = values.astype(jnp.bfloat16)
    low = (values - high.astype(jnp.float32)).astype(jnp.bfloat16)
    return high, low


def dot32(left, right):
    return jnp.dot(left, right, preferred_element_type=jnp.float32)


def np_angles(freqs, positions, length):
    angles = (np.outer(freqs, positions) % length) * (2.0 * math.pi / length)
    return np.cos(angles), np.sin(angles)


def np_split(table):
    high = table.astype(np.float32).astype(ml_dtypes.bfloat16)
    low = (table - high.astype(np.float64)).astype(np.float32).astype(ml_dtypes.bfloat16)
    return high, low


def np_bf16(table):
    return table.astype(np.float32).astype(ml_dtypes.bfloat16)


def make_tables(rows_y, rows_z, steps_t, channels, devices):
    half = KT * channels
    lanes = 2 * half
    eye_c = np.eye(channels)
    cos_z, sin_z = np_angles(np.arange(KZ) - KZ // 2, np.arange(rows_z), rows_z)
    cos_y, sin_y = np_angles(np.arange(KY) - KY // 2, np.arange(rows_y), rows_y)
    cos_t, sin_t = np_angles(np.arange(KT), np.arange(steps_t), steps_t)
    cos_x, sin_x = np_angles(np.arange(KX) - KX // 2, np.arange(devices), devices)
    tables = {}
    tables["z_fwd"] = np_bf16(np.concatenate([cos_z, sin_z], 0))
    tables["y_fwd"] = np_bf16(np.concatenate([cos_y, sin_y], 0))
    time_fwd = np.kron(np.stack([cos_t.T, -sin_t.T], 1).reshape(steps_t, 2 * KT), eye_c)
    turned = np.concatenate([time_fwd[:, half:], -time_fwd[:, :half]], 1)
    tables["t_fwd"] = np_bf16(np.concatenate([time_fwd, turned], 0))
    y_high, y_low = np_split(np.concatenate([cos_y.T, sin_y.T], 1))
    tables["y_back"] = np.concatenate([y_high, y_high, y_low], 1)
    time_back = np.concatenate(
        [np.concatenate([cos_t, sin_t], 1), np.concatenate([-sin_t, cos_t], 1)], 0
    )
    tables["t_back"] = np_bf16(np.kron(time_back, eye_c))
    tables["z_back"] = np_bf16(np.concatenate([cos_z.T, -sin_z.T], 1))
    eye_p = np.eye(PAD_ROWS)

    def spread(base):
        return np.einsum("kx,pq->pkxq", base, eye_p).reshape(
            PAD_ROWS * KX, devices * PAD_ROWS
        )

    x_high, x_low = np_split(np.concatenate([spread(cos_x), spread(sin_x)], 0))
    tables["x_fwd"] = np.concatenate([x_high, x_high, x_low], 1)
    tables["x_back"] = np.concatenate(
        np_split(np.concatenate([spread(cos_x).T, spread(sin_x).T], 1)), 0
    )
    c = channels
    pick_s = np.zeros((KT, 2, KT, c, 2, 2, c, c))
    pick_t = np.zeros((KT, 2, KT, c, 2, 2, c, c))
    fold_s = np.zeros((KT, 2, 2, c, c, 2, KT, c))
    fold_t = np.zeros((KT, 2, 2, c, c, 2, KT, c))
    for k in range(KT):
        for a in range(c):
            pick_s[k, 0, k, a, 0, :, a, :] = 1
            pick_s[k, 1, k, a, 1, 0, a, :] = 1
            pick_s[k, 1, k, a, 1, 1, a, :] = -1
            pick_t[k, 0, k, a, 0, 0, :, a] = 1
            pick_t[k, 1, k, a, 0, 1, :, a] = 1
            pick_t[k, 1, k, a, 1, 0, :, a] = 1
            pick_t[k, 0, k, a, 1, 1, :, a] = 1
            fold_s[k, 0, 0, :, a, 0, k, a] = 1
            fold_s[k, 1, 1, :, a, 0, k, a] = 1
            fold_s[k, 0, 1, :, a, 1, k, a] = 1
            fold_s[k, 1, 0, :, a, 1, k, a] = 1
            fold_t[k, 0, :, a, :, 0, k, a] = 1
            fold_t[k, 1, 0, a, :, 1, k, a] = 1
            fold_t[k, 1, 1, a, :, 1, k, a] = -1
    wide = 2 * c * c

    def doubled(pick):
        flat = pick.reshape(KT, lanes, 2 * wide)
        return np_bf16(np.concatenate([flat, flat], 1))

    tables["pick_s"] = doubled(pick_s)
    tables["pick_t"] = doubled(pick_t)
    tables["fold_s"] = np_bf16(fold_s.reshape(KT, 2 * wide, lanes))
    tables["fold_t"] = np_bf16(fold_t.reshape(KT, 2 * wide, lanes))
    return {name: jnp.asarray(table) for name, table in tables.items()}


def half_sign(shape, first, second):
    lane = lax.broadcasted_iota(jnp.int32, shape, 1)
    return jnp.where(lane < shape[1] // 2, first, second).astype(jnp.float32)


def roll_half(values):
    return pltpu.roll(values, values.shape[1] // 2, 1)


def z_forward(rows, count, z_table, t_table):
    pieces = []
    for y in range(count):
        both = dot32(z_table, rows(y))
        pieces.append(jnp.concatenate([both[:KZ], both[KZ:]], axis=1))
    stacked = jnp.concatenate(pieces, axis=0).astype(jnp.bfloat16)
    return dot32(stacked, t_table)


def y_forward(zbuf, spec, y_table, rows_y, lanes):
    sign = half_sign((KY, lanes), 1.0, -1.0)
    for kz in range(KZ):
        column = zbuf[pl.ds(kz, rows_y, stride=KZ), :].astype(jnp.bfloat16)
        both = dot32(y_table, column)
        spec[pl.ds(kz, KY, stride=KZ), :] = both[:KY] + sign * roll_half(both[KY:])


def y_backward(spec, ubuf, y_table, rows_y, lanes):
    sign = half_sign((KY, lanes), -1.0, 1.0)
    for kz in range(KZ):
        column = spec[pl.ds(kz, KY, stride=KZ), :]
        both = jnp.concatenate([column, sign * roll_half(column)], axis=0)
        high, low = split_pair(both)
        stacked = jnp.concatenate([high, low, high], axis=0)
        ubuf[pl.ds(kz, rows_y, stride=KZ), :] = dot32(y_table, stacked)


def z_backward(ubuf, start, count, t_table):
    lanes = ubuf.shape[1]
    rows = ubuf[pl.ds(start, count * KZ), :].astype(jnp.bfloat16)
    timed = dot32(rows, t_table)
    pieces = []
    for y in range(count):
        mine = timed[y * KZ : (y + 1) * KZ]
        pieces.append(
            jnp.concatenate([mine[:, :lanes], mine[:, lanes:]], axis=0).astype(jnp.bfloat16)
        )
    return pieces


def write_blocks(spec, out_ref, own, stats):
    devices, padded, lanes = out_ref.shape
    spare = padded - own
    if spare > 1:
        zeros = jnp.zeros((spare - 1, lanes), jnp.float32)
        tail = jnp.concatenate([stats, zeros], axis=0)
    else:
        tail = stats
    for d in range(devices):
        out_ref[d, 0:own, :] = spec[d * own : (d + 1) * own, :]
        out_ref[d, own:padded, :] = tail


def read_blocks(in_ref, spec, own, scale):
    for d in range(in_ref.shape[0]):
        spec[d * own : (d + 1) * own, :] = in_ref[d, 0:own, :] * scale


def greet_all():
    devices = lax.axis_size("space")
    me = lax.axis_index("space")
    barrier = pltpu.get_barrier_semaphore()

    def signal(offset, carry):
        peer = lax.rem(me + offset, devices)
        pl.semaphore_signal(
            barrier, inc=1, device_id={"space": peer}, device_id_type=pl.DeviceIdType.MESH
        )
        return carry

    lax.fori_loop(1, devices, signal, 0)


def await_all():
    pl.semaphore_wait(pltpu.get_barrier_semaphore(), lax.axis_size("space") - 1)


def peer_copy(offset, part, rows, send, recv, send_sems, recv_sems):
    devices = lax.axis_size("space")
    me = lax.axis_index("space")
    peer = lax.rem(me + offset, devices)
    low, high = rows
    return pltpu.make_async_remote_copy(
        src_ref=send.at[peer, low:high],
        dst_ref=recv.at[me, low:high],
        send_sem=send_sems.at[part, offset],
        recv_sem=recv_sems.at[part, offset],
        device_id={"space": peer},
        device_id_type=pl.DeviceIdType.MESH,
    )


def each_peer(action, part, rows, buffers):
    def body(offset, carry):
        action(peer_copy(offset, part, rows, *buffers))
        return carry

    lax.fori_loop(1, lax.axis_size("space"), body, 0)


def start_part(part, rows, buffers):
    each_peer(lambda copy: copy.start(), part, rows, buffers)
    send, recv = buffers[:2]
    me = lax.axis_index("space")
    low, high = rows
    recv[me, low:high, :] = send[me, low:high, :]


def row_parts(padded):
    tiles = padded // PAD_ROWS
    cut = max(tiles * 2 // 5, 1)
    parts = [(0, cut), (cut, tiles)] if cut < tiles else [(0, tiles)]
    return parts


def exchange_and_mix(to_owner, to_planes, mix_tile, out_ref):
    padded = to_owner[0].shape[1]
    parts = row_parts(padded)
    rows = [(low * PAD_ROWS, high * PAD_ROWS) for low, high in parts]
    for part in range(len(parts)):
        start_part(part, rows[part], to_owner)
    for part, (low, high) in enumerate(parts):
        each_peer(lambda copy: copy.wait_recv(), part, rows[part], to_owner)
        for tile in range(low, high):
            mix_tile(tile)
        start_part(part, rows[part], to_planes)
    for part in range(len(parts)):
        each_peer(lambda copy: copy.wait_recv(), part, rows[part], to_planes)
    for part in range(len(parts)):
        each_peer(lambda copy: copy.wait_send(), part, rows[part], to_owner)
        each_peer(lambda copy: copy.wait_send(), part, rows[part], to_planes)
    out_ref[...] = to_planes[1][...]


def fetch(sources, targets, sems):
    return [
        pltpu.make_async_copy(source, target, sems.at[index])
        for index, (source, target) in enumerate(zip(sources, targets))
    ]


def mix_one_tile(tile, in_ref, w_ref, tables, spectrum_ref, send_ref):
    xf_ref, xb_ref, pick_ref, fold_ref = tables
    own = w_ref.shape[0]
    rows = PAD_ROWS * KX
    first = tile * PAD_ROWS
    pairs = min(PAD_ROWS, own - first)
    if pairs <= 0:
        send_ref[:, first : first + PAD_ROWS, :] = jnp.zeros(
            (send_ref.shape[0], PAD_ROWS, send_ref.shape[2]), jnp.float32
        )
        return
    spectrum = x_forward(in_ref, tile, xf_ref[...])
    spectrum_ref[tile * rows : (tile + 1) * rows, :] = spectrum
    mixed = mixed_rows(spectrum[: pairs * KX], w_ref, first, pairs, pick_ref, fold_ref)
    x_backward(mixed, send_ref, tile, xb_ref[...])


def repeat_matrix(lanes, channels):
    row = lax.broadcasted_iota(jnp.int32, (lanes, channels), 0)
    column = lax.broadcasted_iota(jnp.int32, (lanes, channels), 1)
    return (row % channels == column).astype(jnp.float32).astype(jnp.bfloat16)


def repeated_table(weight, lanes, flip):
    channels = weight.shape[0]
    repeat = repeat_matrix(lanes, channels)
    inner = lax.dot_general(
        repeat,
        weight,
        (((1,), (1 if flip else 0,)), ((), ())),
        preferred_element_type=jnp.float32,
    ).astype(jnp.bfloat16)
    full = lax.dot_general(
        inner, repeat, (((1,), (1,)), ((), ())), preferred_element_type=jnp.float32
    )
    row = lax.broadcasted_iota(jnp.int32, (lanes, lanes), 0)
    lane = lax.broadcasted_iota(jnp.int32, (lanes, lanes), 1)
    return jnp.where(row // channels == lane // channels, full, 0.0).astype(jnp.bfloat16)


def spectrum_kernel(
    count,
    own,
    f_ref,
    zt_ref,
    tt_ref,
    yt_ref,
    w_hbm,
    xf_ref,
    xb_ref,
    pick_hbm,
    fold_hbm,
    spectrum_ref,
    out_ref,
    zbuf,
    spec,
    send_a,
    recv_a,
    send_b,
    recv_b,
    send_sems_a,
    recv_sems_a,
    send_sems_b,
    recv_sems_b,
    w_ref,
    pick_ref,
    fold_ref,
    fetch_sems,
):
    step = pl.program_id(0)
    fetches = fetch((w_hbm, pick_hbm, fold_hbm), (w_ref, pick_ref, fold_ref), fetch_sems)

    @pl.when(step == 0)
    def _():
        greet_all()
        for copy in fetches:
            copy.start()

    lanes = zbuf.shape[1]
    chunk = z_forward(lambda y: f_ref[y], count, zt_ref[...], tt_ref[...])
    zbuf[pl.ds(pl.multiple_of(step * (count * KZ), 8), count * KZ), :] = chunk

    @pl.when(step == pl.num_programs(0) - 1)
    def _():
        y_forward(zbuf, spec, yt_ref[...], zbuf.shape[0] // KZ, lanes)
        write_blocks(spec, send_a, own, jnp.zeros((1, lanes), jnp.float32))
        await_all()
        for copy in fetches:
            copy.wait()
        tables = (xf_ref, xb_ref, pick_ref, fold_ref)
        exchange_and_mix(
            (send_a, recv_a, send_sems_a, recv_sems_a),
            (send_b, recv_b, send_sems_b, recv_sems_b),
            lambda tile: mix_one_tile(tile, recv_a, w_ref, tables, spectrum_ref, send_b),
            out_ref,
        )


def activation_kernel(
    count,
    own,
    scale,
    channels,
    in_ref,
    f_ref,
    cot_ref,
    skip_ref,
    bias_ref,
    yb_ref,
    tb_ref,
    zb_ref,
    zt_ref,
    tt_ref,
    yt_ref,
    w_hbm,
    xf_ref,
    xb_ref,
    pick_hbm,
    fold_hbm,
    out_ref,
    grad_ref,
    spectrum_ref,
    arrived_ref,
    stats_ref,
    ubuf,
    zbuf,
    spec,
    outer,
    total_row,
    skip_table,
    bias_buf,
    send_a,
    recv_a,
    send_b,
    recv_b,
    send_sems_a,
    recv_sems_a,
    send_sems_b,
    recv_sems_b,
    w_ref,
    pick_ref,
    fold_ref,
    fetch_sems,
):
    step = pl.program_id(0)
    fetches = fetch((w_hbm, pick_hbm, fold_hbm), (w_ref, pick_ref, fold_ref), fetch_sems)
    lanes = ubuf.shape[1]
    rows_y = ubuf.shape[0] // KZ

    @pl.when(step == 0)
    def _():
        greet_all()
        for copy in fetches:
            copy.start()
        skip_table[...] = repeated_table(skip_ref[...], lanes, False)
        bias_buf[...] = lax.dot_general(
            bias_ref[...],
            repeat_matrix(lanes, channels),
            (((1,), (1,)), ((), ())),
            preferred_element_type=jnp.float32,
        )
        read_blocks(in_ref, spec, own, scale)
        y_backward(spec, ubuf, yb_ref[...], rows_y, lanes)
        outer[...] = jnp.zeros_like(outer)
        total_row[...] = jnp.zeros_like(total_row)

    start = pl.multiple_of(step * (count * KZ), 8)
    pieces = z_backward(ubuf, start, count, tb_ref[...])
    bias_row = bias_buf[...]
    for y in range(count):
        field = f_ref[y]
        pre = dot32(zb_ref[...], pieces[y]) + dot32(field, skip_table[...]) + bias_row
        cdf = 0.5 * (1.0 + lax.erf(pre * (1.0 / math.sqrt(2.0))))
        pdf = jnp.exp(-0.5 * pre * pre) * (1.0 / math.sqrt(2.0 * math.pi))
        out_ref[y] = (pre * cdf).astype(jnp.bfloat16)
        slope = cdf + pre * pdf
        grad = (cot_ref[y].astype(jnp.float32) * slope).astype(jnp.bfloat16)
        grad_ref[y] = grad
        total_row[...] += jnp.sum(
            grad.astype(jnp.float32).reshape(-1, 8, lanes), axis=0
        )
    flat_f = f_ref[...].reshape(-1, lanes)
    flat_g = grad_ref[...].reshape(-1, lanes)
    outer[...] += lax.dot_general(
        flat_f, flat_g, (((0,), (0,)), ((), ())), preferred_element_type=jnp.float32
    )
    chunk = z_forward(lambda y: grad_ref[y], count, zt_ref[...], tt_ref[...])
    zbuf[pl.ds(start, count * KZ), :] = chunk

    @pl.when(step == pl.num_programs(0) - 1)
    def _():
        y_forward(zbuf, spec, yt_ref[...], rows_y, lanes)
        row = lax.broadcasted_iota(jnp.int32, (lanes, lanes), 0)
        lane = lax.broadcasted_iota(jnp.int32, (lanes, lanes), 1)
        same_t = row // channels == lane // channels
        same_c = (row % channels == lane % channels).astype(jnp.float32)
        diagonal = jnp.where(same_t, outer[...], 0.0)
        per_c = jnp.dot(diagonal, same_c, precision=FULL_PRECISION)
        keep = (row % channels) == (lane // channels)
        skip_row = jnp.sum(jnp.where(keep, per_c, 0.0), axis=0, keepdims=True)
        folded = jnp.dot(total_row[...], same_c, precision=FULL_PRECISION)
        group = lax.broadcasted_iota(jnp.int32, (1, lanes), 1) // channels
        bias_sum = jnp.sum(folded, axis=0, keepdims=True)
        bias_sum = jnp.where(group == channels, bias_sum, 0.0)
        write_blocks(spec, send_a, own, skip_row + bias_sum)
        await_all()
        for copy in fetches:
            copy.wait()
        tables = (xf_ref, xb_ref, pick_ref, fold_ref)
        exchange_and_mix(
            (send_a, recv_a, send_sems_a, recv_sems_a),
            (send_b, recv_b, send_sems_b, recv_sems_b),
            lambda tile: mix_one_tile(tile, recv_a, w_ref, tables, spectrum_ref, send_b),
            arrived_ref,
        )
        stats_ref[...] = jnp.sum(recv_a[:, own, :], axis=0, keepdims=True)


def field_grad_kernel(
    count,
    own,
    scale,
    root,
    in_ref,
    grad_ref,
    skip_ref,
    stats_ref,
    yb_ref,
    tb_ref,
    zb_ref,
    out_ref,
    skip_out,
    bias_out,
    ubuf,
    spec,
    skip_table,
):
    step = pl.program_id(0)
    lanes = ubuf.shape[1]

    @pl.when(step == 0)
    def _():
        read_blocks(in_ref, spec, own, scale)
        y_backward(spec, ubuf, yb_ref[...], ubuf.shape[0] // KZ, lanes)
        skip_table[...] = repeated_table(skip_ref[...], lanes, True)
        channels = skip_ref.shape[0]
        group = lax.broadcasted_iota(jnp.int32, (2 * channels, lanes), 1) // channels
        row = lax.broadcasted_iota(jnp.int32, (2 * channels, lanes), 0)
        chosen = jnp.where(group == row, stats_ref[...] * root, 0.0)
        fold = repeat_matrix(lanes, channels).astype(jnp.float32)
        folded = jnp.dot(chosen, fold, precision=FULL_PRECISION)
        skip_out[...] = folded[:channels]
        bias_out[...] = folded[channels : channels + 1]

    start = pl.multiple_of(step * (count * KZ), 8)
    pieces = z_backward(ubuf, start, count, tb_ref[...])
    for y in range(count):
        value = dot32(zb_ref[...], pieces[y]) + dot32(grad_ref[y], skip_table[...])
        out_ref[y] = value.astype(jnp.bfloat16)


def x_forward(in_ref, tile, x_table):
    devices, _, lanes = in_ref.shape
    block = in_ref[:, tile * PAD_ROWS : (tile + 1) * PAD_ROWS, :]
    block = block.reshape(devices * PAD_ROWS, lanes)
    high, low = split_pair(block)
    both = dot32(x_table, jnp.concatenate([high, low, high], axis=0))
    rows = PAD_ROWS * KX
    return both[:rows] + half_sign((rows, lanes), 1.0, -1.0) * roll_half(both[rows:])


def x_backward(columns, out_ref, tile, x_table):
    devices, _, lanes = out_ref.shape
    missing = PAD_ROWS * KX - columns.shape[0]
    if missing:
        columns = jnp.concatenate([columns, jnp.zeros((missing, lanes), jnp.float32)], axis=0)
    turned = half_sign(columns.shape, -1.0, 1.0) * roll_half(columns)
    high, low = split_pair(jnp.concatenate([columns, turned], axis=0))
    size = devices * PAD_ROWS
    from_high = dot32(x_table, high)
    rows = from_high[:size] + from_high[size:] + dot32(x_table[:size], low)
    out_ref[:, tile * PAD_ROWS : (tile + 1) * PAD_ROWS, :] = rows.reshape(
        devices, PAD_ROWS, lanes
    )


def mixed_rows(spectrum, w_ref, first, pairs, pick_ref, fold_ref):
    wide = w_ref.shape[3]
    high, low = split_pair(spectrum)
    doubled = jnp.concatenate([high, low], axis=1)
    total = None
    for k in range(KT):
        terms = dot32(doubled, pick_ref[k])
        weight = w_ref[first : first + pairs, k].astype(jnp.float32).reshape(pairs * KX, wide)
        product = jnp.concatenate([terms[:, :wide] * weight, terms[:, wide:] * weight], axis=1)
        part = dot32(product.astype(jnp.bfloat16), fold_ref[k])
        total = part if total is None else total + part
    return total


def weight_gradient_kernel(scale, s_ref, t_ref, ps_ref, pt_ref, out_ref):
    pairs, _, _, wide = out_ref.shape
    for_s = jnp.concatenate(split_pair(s_ref[...]), axis=1)
    for_t = jnp.concatenate(split_pair(t_ref[...] * scale), axis=1)
    for k in range(KT):
        left = dot32(for_s, ps_ref[k])
        right = dot32(for_t, pt_ref[k])
        value = left[:, :wide] * right[:, :wide] + left[:, wide:] * right[:, wide:]
        out_ref[:, k] = value.reshape(pairs, KX, wide)


def whole(array):
    zeros = (0,) * len(array.shape)
    return pl.BlockSpec(array.shape, lambda *_: zeros)


def params(mebibytes, **extra):
    return pltpu.CompilerParams(vmem_limit_bytes=mebibytes * 1024 * 1024, **extra)


def fast_device(field, cotangent, spectral_weight, skip_weight, bias):
    _, rows_y, rows_z, lanes = field.shape
    channels = skip_weight.shape[0]
    steps_t = lanes // channels
    devices = lax.axis_size("space")
    total = devices * rows_y * rows_z * steps_t
    scale = 1.0 / total
    own = KY * KZ // devices
    padded = (own // PAD_ROWS + 1) * PAD_ROWS
    wide = spectral_weight.shape[2]
    t = make_tables(rows_y, rows_z, steps_t, channels, devices)
    count = 32
    while rows_y % count:
        count //= 2
    steps = rows_y // count
    field = field.reshape(rows_y, rows_z, lanes)
    cotangent = cotangent.reshape(rows_y, rows_z, lanes)
    weights = spectral_weight.reshape(own, KT, KX, wide)
    bias_row = bias.reshape(1, channels)
    plane_spec = pl.BlockSpec((count, rows_z, lanes), lambda i: (i, 0, 0))
    plane_shape = jax.ShapeDtypeStruct((rows_y, rows_z, lanes), jnp.bfloat16)
    block_shape = jax.ShapeDtypeStruct((devices, padded, lanes), jnp.float32)
    block_spec = pl.BlockSpec((devices, padded, lanes), lambda *_: (0, 0, 0))
    mode_rows = pl.cdiv(own, PAD_ROWS) * PAD_ROWS * KX
    spectrum_shape = jax.ShapeDtypeStruct((mode_rows, lanes), jnp.float32)
    plane_buf = pltpu.VMEM((rows_y * KZ, lanes), jnp.float32)
    spec_buf = pltpu.VMEM((KY * KZ, lanes), jnp.float32)

    parts = len(row_parts(padded))
    block_buf = pltpu.VMEM((devices, padded, lanes), jnp.float32)
    sems = pltpu.SemaphoreType.DMA((parts, devices))
    link_scratch = [block_buf] * 4 + [sems] * 4
    link_scratch += [
        pltpu.VMEM(x.shape, x.dtype) for x in (weights, t["pick_s"], t["fold_s"])
    ]
    link_scratch += [pltpu.SemaphoreType.DMA((3,))]
    far = pl.BlockSpec(memory_space=pl.ANY)
    mixing_specs = [far, whole(t["x_fwd"]), whole(t["x_back"]), far, far]
    spectrum_spec = pl.BlockSpec(spectrum_shape.shape, lambda *_: (0, 0))
    mixing_s = (weights, t["x_fwd"], t["x_back"], t["pick_s"], t["fold_s"])
    mixing_t = (weights, t["x_fwd"], t["x_back"], t["pick_t"], t["fold_t"])
    operands = (field, t["z_fwd"], t["t_fwd"], t["y_fwd"]) + mixing_s
    own_field, arrived = pl.pallas_call(
        functools.partial(spectrum_kernel, count, own),
        grid=(steps,),
        in_specs=[plane_spec] + [whole(x) for x in operands[1:-5]] + mixing_specs,
        out_specs=[spectrum_spec, block_spec],
        out_shape=[spectrum_shape, block_shape],
        scratch_shapes=[plane_buf, spec_buf] + link_scratch,
        compiler_params=params(60, collective_id=0, has_side_effects=True),
        name="forward_mix",
    )(*operands)
    operands = (
        arrived,
        field,
        cotangent,
        skip_weight,
        bias_row,
        t["y_back"],
        t["t_back"],
        t["z_back"],
        t["z_fwd"],
        t["t_fwd"],
        t["y_fwd"],
    ) + mixing_t
    stats_shape = jax.ShapeDtypeStruct((1, lanes), jnp.float32)
    output, grad_pre, own_grad, arrived, stats = pl.pallas_call(
        functools.partial(activation_kernel, count, own, scale, channels),
        grid=(steps,),
        in_specs=[whole(operands[0]), plane_spec, plane_spec]
        + [whole(x) for x in operands[3:-5]]
        + mixing_specs,
        out_specs=[plane_spec, plane_spec, spectrum_spec, block_spec, whole(stats_shape)],
        out_shape=[plane_shape, plane_shape, spectrum_shape, block_shape, stats_shape],
        scratch_shapes=[
            plane_buf,
            plane_buf,
            spec_buf,
            pltpu.VMEM((lanes, lanes), jnp.float32),
            pltpu.VMEM((8, lanes), jnp.float32),
            pltpu.VMEM((lanes, lanes), jnp.bfloat16),
            pltpu.VMEM((1, lanes), jnp.float32),
        ]
        + link_scratch,
        compiler_params=params(60, collective_id=1, has_side_effects=True),
        name="activation_mix",
    )(*operands)
    pairs = 12 if own % 12 == 0 else 1
    mode_spec = pl.BlockSpec((pairs * KX, lanes), lambda i: (i, 0))
    spectral_grad = pl.pallas_call(
        functools.partial(weight_gradient_kernel, scale),
        grid=(own // pairs,),
        in_specs=[mode_spec, mode_spec, whole(t["pick_s"]), whole(t["pick_t"])],
        out_specs=pl.BlockSpec((pairs, KT, KX, wide), lambda i: (i, 0, 0, 0)),
        out_shape=jax.ShapeDtypeStruct((own, KT, KX, wide), jnp.float32),
        compiler_params=params(48),
        cost_estimate=pl.CostEstimate(
            flops=4 * own * KX * KT * 65536, bytes_accessed=8 * own * KX * KT * wide, transcendentals=0
        ),
        name="weight_gradient",
    )(own_field, own_grad, t["pick_s"], t["pick_t"])
    operands = (arrived, grad_pre, skip_weight, stats, t["y_back"], t["t_back"], t["z_back"])
    root = 1.0 / math.sqrt(total)
    square_shape = jax.ShapeDtypeStruct((channels, channels), jnp.float32)
    line_shape = jax.ShapeDtypeStruct((1, channels), jnp.float32)
    field_grad, skip_grad, bias_grad = pl.pallas_call(
        functools.partial(field_grad_kernel, count, own, scale, root),
        grid=(steps,),
        in_specs=[whole(operands[0]), plane_spec] + [whole(x) for x in operands[2:]],
        out_specs=[plane_spec, whole(square_shape), whole(line_shape)],
        out_shape=[plane_shape, square_shape, line_shape],
        scratch_shapes=[plane_buf, spec_buf, pltpu.VMEM((lanes, lanes), jnp.bfloat16)],
        compiler_params=params(48),
        name="field_grad",
    )(*operands)
    return (
        output[None],
        field_grad[None],
        spectral_grad.reshape(own * KT, KX, wide),
        skip_grad,
        bias_grad.reshape(channels),
    )


def on_any_device(field, cotangent, spectral_weight, skip_weight, bias):
    devices = lax.axis_size("space")
    channels = skip_weight.shape[0]
    fits = (
        field.shape[0] == 1
        and (KY * KZ) % devices == 0
        and devices <= 32
        and field.shape[3] == 2 * KT * channels
        and channels * channels + channels <= field.shape[3]
        and spectral_weight.shape[2] == field.shape[3]
    )
    body = fast_device if fits else on_device
    return body(field, cotangent, spectral_weight, skip_weight, bias)


def solution(mesh):
    in_specs = (
        P(("groups", "space"), None, None, None),
        P(("groups", "space"), None, None, None),
        P("space", None, None),
        P(),
        P(),
    )
    out_specs = (
        P(("groups", "space"), None, None, None),
        P(("groups", "space"), None, None, None),
        P(("groups", "space"), None, None),
        P("groups", None),
        P("groups"),
    )
    return jax.shard_map(
        on_any_device, mesh=mesh, in_specs=in_specs, out_specs=out_specs, check_vma=False
    )
```
